32 devices in a mesh: fsdp: 2 (over x), context: 4 (over z), tensor: 4 (over y, core).
Axes of the slice: x: 2, y: 2, z: 4, core: 2. Of those that a mesh axis runs over, the one named last changes fastest.
Arguments:
- tokens: bfloat16 [2, 640, 1024], P('fsdp', 'context'), may hold values from -6 to 6
- cotangent: bfloat16 [2, 640, 1024], P('fsdp', 'context'), may hold values from -6 to 6
- valid_count: int32 [2], P('fsdp'), may hold values from 481 to 640, as said below
- gain_first: bfloat16 [1024], P('fsdp'), may hold values from 0.5 to 1.5
- shift_first: bfloat16 [1024], P('fsdp'), may hold values from -1.75 to 1.75
- query_weight: bfloat16 [1024, 1024], P('fsdp', 'tensor'), may hold values from -0.25 to 0.25
- query_bias: bfloat16 [64, 16], P('fsdp', 'tensor'), may hold values from -1.75 to 1.75
- key_weight: bfloat16 [1024, 1024], P('fsdp', 'tensor'), may hold values from -0.25 to 0.25
- value_weight: bfloat16 [1024, 1024], P('fsdp', 'tensor'), may hold values from -0.1875 to 0.1875
- value_bias: bfloat16 [64, 16], P('fsdp', 'tensor'), may hold values from -1.75 to 1.75
- output_weight: bfloat16 [1024, 1024], P('tensor', 'fsdp'), may hold values from -0.5 to 0.5
- output_bias: bfloat16 [1024], P('fsdp'), may hold values from -1.75 to 1.75
- gain_second: bfloat16 [1024], P('fsdp'), may hold values from 0.5 to 1.5
- shift_second: bfloat16 [1024], P('fsdp'), may hold values from -1.75 to 1.75
- expand_weight: bfloat16 [1024, 4096], P('fsdp', 'tensor'), may hold values from -0.1875 to 0.1875
- expand_bias: bfloat16 [128, 32], P('fsdp', 'tensor'), may hold values from -1.75 to 1.75
- reduce_weight: bfloat16 [4096, 1024], P('tensor', 'fsdp'), may hold values from -0.09375 to 0.09375
- reduce_bias: bfloat16 [1024], P('fsdp'), may hold values from -1.75 to 1.75
Outputs:
- output: bfloat16 [2, 640, 1024], P('fsdp', 'context')
- grad_tokens: float32 [2, 640, 1024], P('fsdp', 'context')
- grad_gain_first: float32 [1024], P('fsdp')
- grad_shift_first: float32 [1024], P('fsdp')
- grad_query_weight: float32 [1024, 1024], P('fsdp', 'tensor')
- grad_query_bias: float32 [64, 16], P('fsdp', 'tensor')
- grad_key_weight: float32 [1024, 1024], P('fsdp', 'tensor')
- grad_value_weight: float32 [1024, 1024], P('fsdp', 'tensor')
- grad_value_bias: float32 [64, 16], P('fsdp', 'tensor')
- grad_output_weight: float32 [1024, 1024], P('tensor', 'fsdp')
- grad_output_bias: float32 [1024], P('fsdp')
- grad_gain_second: float32 [1024], P('fsdp')
- grad_shift_second: float32 [1024], P('fsdp')
- grad_expand_weight: float32 [1024, 4096], P('fsdp', 'tensor')
- grad_expand_bias: float32 [128, 32], P('fsdp', 'tensor')
- grad_reduce_weight: float32 [4096, 1024], P('tensor', 'fsdp')
- grad_reduce_bias: float32 [1024], P('fsdp')
The draws below stay inside these ranges and needn't reach their ends.
Inputs may be any that keep to these rules, and one draw needn't show every extreme that they name: `valid_count`: some image, drawn from the seed, has all 640 positions valid; every image has more than three quarters of 640 valid.
All inputs are finite; a program needn't handle non-finite values.
Results may differ from the reference program's by a relative error of at most 0.025.
Values may be sent and summed in bfloat16 or wider, within the bound.
No kernel may reach another device: no remote copies, remote signals or barrier semaphores. Data moves between devices by JAX's collectives and lax.ppermute only.
A program may use at most 128 MiB of HBM per device.

```python
import jax
import jax.numpy as jnp
from jax import lax

D = 1024
H = 16
HD = 64
FF = 4096
LEN = 640
IMAGES = 2


def draw_valid_count(key, part):
    key = jax.random.fold_in(key, 7)
    count_key, pick_key = jax.random.split(key)
    counts = jax.random.randint(count_key, (IMAGES,), LEN - LEN // 4 + 1, LEN + 1)
    order = jax.random.permutation(pick_key, IMAGES)
    chosen = jnp.arange(IMAGES, dtype=jnp.int32) == order[0]
    counts = jnp.where(chosen, LEN, counts)
    return counts.astype(jnp.int32)


def spiked(values, stream_key, source, target, shards_of, factor):
    def block_of(position):
        return (jnp.arange(values.shape[position]) // (values.shape[position] // shards_of)).reshape((-1,) + (1,) * (values.ndim - 1 - position))

    near = jax.random.permutation(stream_key, shards_of)[block_of(target)]
    second = (block_of(target) + shards_of // 2) % shards_of
    return jnp.where((block_of(source) == near) | (block_of(source) == second), factor * values, values)


def block_scale(own_key, dims, pieces, least, high):
    factor_of = 1.0
    for axis_at, parts in pieces:
        draws = jax.random.uniform(jax.random.fold_in(jax.random.fold_in(own_key, 6), axis_at), (parts,), jnp.float32, least / len(pieces), high / len(pieces))
        factor_of = factor_of * jnp.repeat(jnp.exp(draws), dims[axis_at] // parts).reshape((-1,) + (1,) * (len(dims) - 1 - axis_at))
    return factor_of


def normal_values(own_key, shape, deviation, bound, shards=(), kind=jnp.bfloat16):
    loudness = block_scale(own_key, shape, shards, -0.22, 0.18) if shards else 1.0
    array = jax.random.normal(own_key, shape, jnp.float32) * deviation * loudness
    return jnp.minimum(jnp.maximum(array, -bound), bound).astype(kind)


def noise_with(rng, extent, deviation, limit, cuts, heavy, kind=jnp.bfloat16):
    drawn = deviation * jax.random.normal(rng, extent, jnp.float32)
    if cuts:
        drawn = drawn * block_scale(rng, extent, cuts, -0.22, 0.18)
    return jnp.clip(spiked(drawn, jax.random.fold_in(rng, 3), *heavy), -limit, limit).astype(kind)


def setup_inputs(seed: int = 0) -> dict:
    key_list = jax.random.split(jax.random.key(seed), 19)
    return {
        "tokens": normal_values(key_list[0], (IMAGES, LEN, D), 1.0, 6.0, ((0, 2), (1, 4))),
        "cotangent": noise_with(key_list[1], (IMAGES, LEN, D), 1.0, 6.0, ((0, 2), (1, 4)), (0, 2, 2, 2.0)),
        "valid_count": draw_valid_count(jax.random.fold_in(key_list[18], 71), 0),
        "gain_first": jnp.clip(1.0 + 0.1 * jax.random.normal(key_list[3], (D,), jnp.float32), 0.5, 1.5).astype(jnp.bfloat16),
        "shift_first": normal_values(key_list[4], (D,), 0.3, 1.75, ((0, 2),)),
        "query_weight": normal_values(key_list[5], (D, D), (D // 2) ** -0.5, 0.25, ((0, 2), (1, 4))),
        "query_bias": normal_values(key_list[6], (HD, H), 0.3, 1.75, ((0, 2), (1, 4))),
        "key_weight": normal_values(key_list[7], (D, D), (D // 2) ** -0.5, 0.25, ((0, 2), (1, 4))),
        "value_weight": normal_values(key_list[8], (D, D), D ** -0.5, 0.1875, ((0, 2), (1, 4))),
        "value_bias": normal_values(key_list[9], (HD, H), 0.3, 1.75, ((0, 2), (1, 4))),
        "output_weight": normal_values(key_list[10], (D, D), (D // 8) ** -0.5, 0.5, ((0, 4), (1, 2))),
        "output_bias": normal_values(key_list[11], (D,), 0.3, 1.75, ((0, 2),)),
        "gain_second": jnp.clip(1.0 + 0.1 * jax.random.normal(key_list[12], (D,), jnp.float32), 0.5, 1.5).astype(jnp.bfloat16),
        "shift_second": normal_values(key_list[13], (D,), 0.3, 1.75, ((0, 2),)),
        "expand_weight": normal_values(key_list[14], (D, FF), D ** -0.5, 0.1875, ((0, 2), (1, 4))),
        "expand_bias": normal_values(key_list[15], (128, FF // 128), 0.3, 1.75, ((0, 2), (1, 4))),
        "reduce_weight": normal_values(key_list[16], (FF, D), FF ** -0.5, 0.09375, ((0, 4), (1, 2))),
        "reduce_bias": normal_values(key_list[17], (D,), 0.3, 1.75, ((0, 2),)),
    }


EPS = 1e-06
HIGH = lax.Precision.HIGHEST

@jax.custom_vjp
def low(v):
    return lax.optimization_barrier(v.astype(jnp.bfloat16)).astype(jnp.float32)

@jax.custom_vjp
def low_back(v):
    return v

def low_keep(v):
    return (low(v), None)

def low_pass(kept, grad):
    return (grad,)

def back_keep(v):
    return (v, None)

def back_low(kept, grad):
    return (low(grad),)
low.defvjp(low_keep, low_pass)
low_back.defvjp(back_keep, back_low)

def matmul(left, right):
    return jnp.dot(left, right, precision=HIGH)

def layer_norm(values, gain, shift):
    center = values - lax.optimization_barrier(jnp.mean(values, -1, keepdims=True))
    spread = lax.optimization_barrier(jnp.mean(center * center, -1, keepdims=True))
    return center * lax.rsqrt(spread + EPS) * gain + shift

def attend(packed):
    queries, keys, values, count = packed
    scale = queries.shape[-1] ** (-0.5)
    scores = jnp.einsum('snd,jnd->nsj', queries, keys, precision=HIGH) * scale
    valid = jnp.arange(keys.shape[0], dtype=jnp.int32)[None, None, :] < count
    scores = low_back(jnp.where(valid, scores, -1e+30))
    top = lax.optimization_barrier(jnp.max(scores, -1, keepdims=True))
    weights = jnp.exp(scores - top)
    weights = low(weights / lax.optimization_barrier(jnp.sum(weights, -1, keepdims=True)))
    return jnp.einsum('nsj,jnd->snd', weights, values, precision=HIGH)

def make_forward(valid_count):

    def forward(tokens, gain_first, shift_first, query_weight, query_bias, key_weight, value_weight, value_bias, output_weight, output_bias, gain_second, shift_second, expand_weight, expand_bias, reduce_weight, reduce_bias):
        images, length, width = tokens.shape
        head_dim, heads = query_bias.shape
        inputs = tokens.reshape(-1, width)
        normed = low(layer_norm(inputs, gain_first, shift_first))
        queries = low_back(low(matmul(normed, query_weight) + query_bias.T.reshape(-1)))
        keys = low_back(low(matmul(normed, key_weight)))
        values = low_back(low(matmul(normed, value_weight) + value_bias.T.reshape(-1)))
        shape = (images, length, heads, head_dim)
        attended = lax.map(jax.checkpoint(attend), (queries.reshape(shape), keys.reshape(shape), values.reshape(shape), valid_count))
        context = low_back(low(attended.reshape(-1, width)))
        branch = low_back(matmul(context, output_weight) + output_bias)
        hidden = inputs + branch
        normed_two = low(layer_norm(hidden, gain_second, shift_second))
        expanded = low_back(matmul(normed_two, expand_weight) + expand_bias.T.reshape(-1))
        activated = low(jax.nn.gelu(expanded, approximate=False))
        reduced = low_back(matmul(activated, reduce_weight) + reduce_bias)
        return (hidden + reduced).reshape(tokens.shape)
    return forward

def reference(tokens, cotangent, valid_count, gain_first, shift_first, query_weight, query_bias, key_weight, value_weight, value_bias, output_weight, output_bias, gain_second, shift_second, expand_weight, expand_bias, reduce_weight, reduce_bias):
    floats = [item.astype(jnp.float32) for item in (tokens, gain_first, shift_first, query_weight, query_bias, key_weight, value_weight, value_bias, output_weight, output_bias, gain_second, shift_second, expand_weight, expand_bias, reduce_weight, reduce_bias)]
    output, pull = jax.vjp(make_forward(valid_count), *floats)
    grads = pull(cotangent.astype(jnp.float32))
    return (output.astype(jnp.bfloat16), grads[0], grads[1], grads[2], grads[3], grads[4], grads[5], grads[6], grads[7], grads[8], grads[9], grads[10], grads[11], grads[12], grads[13], grads[14], grads[15])
```

```python
import jax
import jax.numpy as jnp
from jax import lax
from jax.sharding import PartitionSpec as P

EPS = 1e-06
LOW = jnp.bfloat16
WIDE = jnp.float32


def swap(block, axis, bit):
    return lax.ppermute(block, axis, [(i, i ^ bit) for i in range(lax.axis_size(axis))])


def after(value, *others):
    return lax.optimization_barrier((value, *others))[0]


def pin(value):
    return lax.optimization_barrier(value)


def dot(left, right):
    return lax.dot_general(left, right, (((1,), (0,)), ((), ())), preferred_element_type=WIDE)


def dot_rt(left, right):
    return lax.dot_general(left, right, (((1,), (1,)), ((), ())), preferred_element_type=WIDE)


def dot_lt(left, right):
    return lax.dot_general(left, right, (((0,), (0,)), ((), ())), preferred_element_type=WIDE)


def segments(value, count):
    size = value.shape[1] // count
    return [value[:, i * size : (i + 1) * size] for i in range(count)]


def from_width(value, parts):
    return sum(dot(s, p) for s, p in zip(segments(value, len(parts)), parts))


def to_width(value, parts):
    return jnp.concatenate([dot(value, p) for p in parts], 1)


def from_width_rt(value, parts):
    return sum(dot_rt(s, p) for s, p in zip(segments(value, len(parts)), parts))


def to_width_rt(value, parts):
    return jnp.concatenate([dot_rt(value, p) for p in parts], 1)


def stats(values):
    center = values - jnp.mean(values, -1, keepdims=True)
    return center, lax.rsqrt(jnp.mean(center * center, -1, keepdims=True) + EPS)


def norm_back(xhat, spread, gain, upstream):
    z = upstream * gain
    mean_z = jnp.mean(z, -1, keepdims=True)
    mean_zx = jnp.mean(z * xhat, -1, keepdims=True)
    return (
        spread * (z - mean_z - xhat * mean_zx),
        jnp.sum(upstream * xhat, 0),
        jnp.sum(upstream, 0),
    )


def reorder(blocks, index):
    bit = 1
    while bit < len(blocks):
        flip = (index & bit) != 0
        blocks = [jnp.where(flip, blocks[k ^ bit], blocks[k]) for k in range(len(blocks))]
        bit *= 2
    return blocks


def sum_tensor(value):
    bit = 1
    while bit < lax.axis_size("tensor"):
        value = pin(value)
        value = value.astype(WIDE) + swap(value, "tensor", bit).astype(WIDE)
        bit *= 2
        if bit < lax.axis_size("tensor"):
            value = value.astype(LOW)
    return value


def all_to_all_context(blocks):
    count = len(blocks)
    bit = 1
    blocks = list(blocks)
    while bit < count:
        sent = [k for k in range(count) if k & bit]
        rows = blocks[0].shape[0]
        got = swap(jnp.concatenate([blocks[k] for k in sent], 0), "context", bit)
        for n, k in enumerate(sent):
            blocks[k] = got[n * rows : (n + 1) * rows]
        bit *= 2
    return blocks


def gather_context(block):
    return [block] + [swap(block, "context", k) for k in range(1, lax.axis_size("context"))]


def sum_context(keep, send, place, axis):
    got = swap(send, "context", 1)
    part = pin((keep + got.astype(WIDE)).astype(LOW))
    far = swap(part, "context", 2)
    total = pin((part.astype(WIDE) + far.astype(WIDE)).astype(LOW))
    other = swap(total, "context", 1)
    odd = (place & 1) != 0
    return jnp.concatenate(
        [jnp.where(odd, other, total), jnp.where(odd, total, other)], axis
    ).astype(WIDE)


def halves(value, axis, odd):
    low, high = jnp.split(value, 2, axis)
    return jnp.where(odd, high, low), jnp.where(odd, low, high)


def on_device(
    tokens,
    cotangent,
    valid_count,
    gain_first,
    shift_first,
    query_weight,
    query_bias,
    key_weight,
    value_weight,
    value_bias,
    output_weight,
    output_bias,
    gain_second,
    shift_second,
    expand_weight,
    expand_bias,
    reduce_weight,
    reduce_bias,
):
    images, seq, width = tokens.shape
    ways = lax.axis_size("fsdp")
    pair = ways == 2
    cycle = lax.axis_size("context")
    mine = lax.axis_index("fsdp")
    place = lax.axis_index("context")
    lane = lax.axis_index("tensor")
    odd = (place & 1) != 0
    share = gain_first.shape[0]
    heads_here = query_bias.shape[1]
    head_dim = query_bias.shape[0] * ways
    features = heads_here * head_dim
    group = features // cycle
    scale = head_dim ** (-0.5)
    second = mine == 1

    def turned(value):
        if not pair:
            return value
        low, high = jnp.split(value, 2, -1)
        return jnp.where(second, jnp.concatenate([high, low], -1), value)

    def whole(own, got):
        return jnp.where(
            second, jnp.concatenate([got, own], 0), jnp.concatenate([own, got], 0)
        )

    def head_columns(weight):
        return lax.dynamic_slice_in_dim(weight, place * group, group, 1)

    local = tokens.reshape(seq, width)
    upstream_low = turned(cotangent.reshape(seq, width))

    half = seq // 2
    core = lane & 1
    piece = lax.dynamic_slice_in_dim(local, core * half, half, 0)
    got = jnp.concatenate(gather_context(piece)[1:], 0)

    head_weight = jnp.concatenate(
        [head_columns(w) for w in (query_weight, key_weight, value_weight)], 1
    )
    if pair:
        vectors = (
            gain_first,
            shift_first,
            output_bias,
            gain_second,
            shift_second,
            reduce_bias,
            query_bias.reshape(-1),
            value_bias.reshape(-1),
            expand_bias.reshape(-1),
        )
        flat = jnp.concatenate(vectors)
        columns = head_weight.shape[1]
        lines = -(-flat.shape[0] // columns)
        lines += -lines % 16
        flat = jnp.pad(flat, (0, lines * columns - flat.shape[0])).reshape(lines, columns)
        first = swap(jnp.concatenate([head_weight, flat], 0), "fsdp", 1)
        head_parts = (head_weight, first[:share])
        taken = first[share:].reshape(-1)
        theirs = []
        at = 0
        for v in vectors:
            theirs.append(taken[at : at + v.shape[0]])
            at += v.shape[0]
        gain_one, shift_one, outb_full, gain_two, shift_two, rbias_full = (
            jnp.concatenate([a, b]).astype(WIDE) for a, b in zip(vectors[:6], theirs[:6])
        )
        qbias_full, vbias_full, ebias_full = (
            whole(a, b.reshape(a.shape)).astype(WIDE)
            for a, b in zip((query_bias, value_bias, expand_bias), theirs[6:])
        )
    else:
        gather = lambda v, axis=0: lax.all_gather(v, "fsdp", axis=axis, tiled=True)
        head_parts = (gather(head_weight),)
        gain_one, shift_one, outb_full, gain_two, shift_two, rbias_full = (
            gather(v).astype(WIDE)
            for v in (gain_first, shift_first, output_bias, gain_second, shift_second, reduce_bias)
        )
        qbias_full, vbias_full, ebias_full = (
            gather(v).astype(WIDE) for v in (query_bias, value_bias, expand_bias)
        )

    theirs_rows = swap(got, "tensor", 1)
    upper = core == 1
    blocks = [local]
    for k in range(cycle - 1):
        a, b = got[k * half : (k + 1) * half], theirs_rows[k * half : (k + 1) * half]
        blocks += [jnp.where(upper, b, a), jnp.where(upper, a, b)]
    every = turned(jnp.concatenate(blocks, 0)).astype(WIDE)
    center, spread = stats(every)
    xhat_all = center * spread
    normed_all = (xhat_all * gain_one + shift_one).astype(LOW)

    head_bias = jnp.concatenate(
        [
            head_columns(qbias_full.T.reshape(1, -1)),
            jnp.zeros((1, group), WIDE),
            head_columns(vbias_full.T.reshape(1, -1)),
        ],
        1,
    )
    qkv = (from_width(normed_all, head_parts) + head_bias).astype(LOW)
    positions = jnp.concatenate(
        [(place ^ k) * seq + jnp.arange(seq, dtype=jnp.int32) for k in range(cycle)]
    )
    valid = (positions < valid_count[0])[None, :]
    kept = []
    attended = []
    for h in range(group // head_dim):
        q, k, v = (
            qkv[:, n * group + h * head_dim : n * group + (h + 1) * head_dim] for n in range(3)
        )
        scores = jnp.where(valid, dot_rt(q, k) * scale, -1e30)
        top = jnp.max(scores, -1, keepdims=True)
        raw = jnp.exp(scores - top)
        weights = raw / jnp.sum(raw, -1, keepdims=True)
        probs = weights.astype(LOW)
        attended.append(dot(probs, v))
        kept.append((q, k, v, weights, probs))
    context_all = jnp.concatenate(attended, 1).astype(LOW)
    rows_of = lambda value: [value[k * seq : (k + 1) * seq] for k in range(cycle)]
    context = jnp.concatenate(reorder(all_to_all_context(rows_of(context_all)), place), 1)

    if pair:
        cot_own, cot_other = segments(upstream_low, 2)
        bundle = swap(
            after(jnp.concatenate([output_weight, cot_other], 0), first), "fsdp", 1
        )
        output_parts = (output_weight, bundle[:features])
        cot_got = bundle[features:]
        expand_parts = (expand_weight, swap(after(expand_weight, first), "fsdp", 1))
        reduce_parts = (reduce_weight, swap(after(reduce_weight, qkv), "fsdp", 1))
        qkv_here = jnp.concatenate([query_weight, key_weight, value_weight], 1)
        qkv_parts = (qkv_here, swap(after(qkv_here, context), "fsdp", 1))
    else:
        output_parts = (gather(output_weight, 1),)
        expand_parts = (gather(expand_weight),)
        reduce_parts = (gather(reduce_weight, 1),)
        qkv_parts = (gather(jnp.concatenate([query_weight, key_weight, value_weight], 1)),)

    inputs = turned(local).astype(WIDE)
    branch = sum_tensor(to_width(context, output_parts).astype(LOW)) + outb_full
    hidden = inputs + branch
    center_two, spread_two = stats(hidden)
    xhat_two = center_two * spread_two
    normed_two = (xhat_two * gain_two + shift_two).astype(LOW)
    expanded = from_width(normed_two, expand_parts) + ebias_full.T.reshape(-1)
    cdf = 0.5 * (1.0 + lax.erf(expanded * (2.0**-0.5)))
    activated = (expanded * cdf).astype(LOW)
    slope = cdf + expanded * jnp.exp(-0.5 * expanded * expanded) * 0.3989422804014327
    grad_expanded = (from_width_rt(upstream_low, reduce_parts) * slope).astype(LOW)

    grad_normed_two = sum_tensor(to_width_rt(grad_expanded, expand_parts).astype(LOW))

    if pair:
        near, other = segments(normed_two, 2)
        moved = swap(jnp.concatenate([activated, other], 1), "fsdp", 1)
        units = activated.shape[1]
        act_rows = jnp.concatenate([activated, moved[:, :units]], 0)
        cot_rows = jnp.concatenate([cot_own, cot_got], 0)
        act_keep, act_send = halves(act_rows, 1, odd)
        reduce_send = dot_lt(act_send, cot_rows).astype(LOW)
        reduce_keep = dot_lt(act_keep, cot_rows)
        norm_rows = jnp.concatenate([near, moved[:, units:]], 0)
        ge_rows = jnp.concatenate([grad_expanded, swap(grad_expanded, "fsdp", 1)], 0)
        ge_keep, ge_send = halves(ge_rows, 1, odd)
        expand_send = dot_lt(norm_rows, ge_send).astype(LOW)
        expand_keep = dot_lt(norm_rows, ge_keep)
    else:
        scatter = lambda v, axis: lax.psum_scatter(
            v.astype(LOW), "fsdp", scatter_dimension=axis, tiled=True
        )
        reduce_keep, reduce_send = halves(scatter(dot_lt(activated, upstream_low), 1), 0, odd)
        expand_keep, expand_send = halves(scatter(dot_lt(normed_two, grad_expanded), 0), 1, odd)
    grad_reduce = sum_context(reduce_keep, reduce_send, place, 0)
    grad_expand = sum_context(expand_keep, expand_send, place, 1)

    upstream = upstream_low.astype(WIDE)
    grad_hidden, gain_two_sum, shift_two_sum = norm_back(
        xhat_two, spread_two, gain_two, grad_normed_two
    )
    grad_hidden = grad_hidden + upstream
    grad_branch = pin(grad_hidden.astype(LOW))
    grad_context = from_width_rt(grad_branch, output_parts).astype(LOW)
    grad_heads = all_to_all_context(
        reorder([grad_context[:, k * group : (k + 1) * group] for k in range(cycle)], place)
    )
    grad_all = jnp.concatenate(grad_heads, 0)
    pieces = []
    for h, (q, k, v, weights, probs) in enumerate(kept):
        g = grad_all[:, h * head_dim : (h + 1) * head_dim]
        grad_probs = dot_rt(g, v)
        delta = jnp.sum(weights * grad_probs, -1, keepdims=True)
        grad_scores = (weights * (grad_probs - delta)).astype(LOW)
        pieces.append((dot(grad_scores, k) * scale, dot_lt(grad_scores, q) * scale, dot_lt(probs, g)))
    grad_qkv = pin(
        jnp.concatenate([p[n] for n in range(3) for p in pieces], 1).astype(LOW)
    )

    home = reorder(all_to_all_context(rows_of(grad_qkv)), place)
    home = jnp.concatenate(
        [b[:, n * group : (n + 1) * group] for n in range(3) for b in home], 1
    )
    grad_normed_one = sum_tensor(to_width_rt(home, qkv_parts).astype(LOW))
    center_one, spread_one = stats(inputs)
    grad_inputs, gain_one_sum, shift_one_sum = norm_back(
        center_one * spread_one, spread_one, gain_one, grad_normed_one
    )
    grad_tokens = turned(grad_inputs + grad_hidden).reshape(tokens.shape)

    reduced = sum_tensor(to_width(activated, reduce_parts).astype(LOW)) + rbias_full
    output = turned((hidden + reduced).astype(LOW)).reshape(tokens.shape)

    sums = (
        jnp.sum(grad_branch.astype(WIDE), 0),
        gain_two_sum,
        shift_two_sum,
        jnp.sum(upstream, 0),
    )
    unit_sum = jnp.sum(grad_expanded.astype(WIDE), 0)
    if pair:
        gb_own, gb_other = segments(grad_branch, 2)
        lines = [s.reshape(2, 1, -1) for s in sums]
        unit_lines = unit_sum.reshape(-1, share)
        bottom = [jnp.concatenate([s[n] for s in lines] + [unit_lines], 0) for n in range(2)]
        fill = -(features + bottom[0].shape[0]) % 32
        filler = jnp.zeros((fill, share), WIDE)
        own = jnp.concatenate([dot_lt(context, gb_own), bottom[0], filler], 0)
        away = jnp.concatenate([dot_lt(context, gb_other), bottom[1], filler], 0)
        own = own + swap(away.astype(LOW), "fsdp", 1).astype(WIDE)
    else:
        bottom = [scatter(s, 0).reshape(1, -1) for s in sums]
        unit_lines = lax.psum(unit_sum.astype(LOW), "fsdp").reshape(-1, share)
        own = jnp.concatenate(
            [scatter(dot_lt(context, grad_branch), 1)] + bottom + [unit_lines], 0
        )
        own = jnp.pad(own, ((0, -own.shape[0] % 32), (0, 0))).astype(WIDE)
    keep, send = halves(own, 0, odd)
    own = sum_context(keep, send.astype(LOW), place, 0)
    grad_output = own[:features]
    grad_outb, grad_gain_two, grad_shift_two, grad_rbias = (own[features + n] for n in range(4))
    unit_total = own[features + 4 : features + 4 + unit_lines.shape[0]].reshape(-1)

    def own_rows(value):
        size = value.shape[0] // ways
        return lax.dynamic_slice_in_dim(value, mine * size, size, 0)

    grad_ebias = own_rows(unit_total.reshape(-1, expand_bias.shape[0] * ways).T)

    head_sum = jnp.sum(grad_qkv.astype(WIDE), 0, keepdims=True)
    head_sum = jnp.pad(head_sum, ((0, 15), (0, 0)))
    if pair:
        own_columns, other_columns = segments(normed_all, 2)
        away = jnp.concatenate([dot_lt(other_columns, grad_qkv), head_sum], 0).astype(LOW)
        own = jnp.concatenate([dot_lt(own_columns, grad_qkv), head_sum], 0)
        own = own + swap(away, "fsdp", 1).astype(WIDE)
    else:
        own = jnp.concatenate(
            [scatter(dot_lt(normed_all, grad_qkv), 0), lax.psum(head_sum.astype(LOW), "fsdp")], 0
        )
    heads = reorder(gather_context(pin(own.astype(LOW))), place)
    grad_query, grad_key, grad_value = (
        jnp.concatenate([b[:, n * group : (n + 1) * group] for b in heads], 1).astype(WIDE)
        for n in range(3)
    )
    grad_qbias, grad_vbias = (
        own_rows(g[share].reshape(heads_here, head_dim).T) for g in (grad_query, grad_value)
    )

    last = turned(jnp.stack([gain_one_sum, shift_one_sum]))
    last = jnp.sum(lax.all_gather(last.astype(LOW), ("fsdp", "context")).astype(WIDE), 0)
    last = lax.dynamic_slice_in_dim(last, mine * share, share, 1)
    return (
        output,
        grad_tokens,
        last[0],
        last[1],
        grad_query[:share],
        grad_qbias,
        grad_key[:share],
        grad_value[:share],
        grad_vbias,
        grad_output,
        grad_outb,
        grad_gain_two,
        grad_shift_two,
        grad_expand,
        grad_ebias,
        grad_reduce,
        grad_rbias,
    )


def solution(mesh):
    rows = P("fsdp", "context", None)
    vector = P("fsdp")
    split = P("fsdp", "tensor")
    turned = P("tensor", "fsdp")
    in_specs = (rows, rows, vector, vector, vector, split, split, split, split, split)
    in_specs += (turned, vector, vector, vector, split, split, turned, vector)
    out_specs = (rows, rows, vector, vector, split, split, split, split, split)
    out_specs += (turned, vector, vector, vector, split, split, turned, vector)
    return jax.shard_map(
        on_device, mesh=mesh, in_specs=in_specs, out_specs=out_specs, check_vma=False
    )
```

```python
import jax
import jax.numpy as jnp
from jax import lax
from jax.experimental import pallas as pl
from jax.experimental.pallas import tpu as pltpu
from jax.sharding import PartitionSpec as P

EPS = 1e-06
LOW = jnp.bfloat16
WIDE = jnp.float32


def swap(block, axis, bit):
    return lax.ppermute(block, axis, [(i, i ^ bit) for i in range(lax.axis_size(axis))])


def after(value, *others):
    return lax.optimization_barrier((value, *others))[0]


def pin(value):
    return lax.optimization_barrier(value)


def dot(left, right):
    return lax.dot_general(left, right, (((1,), (0,)), ((), ())), preferred_element_type=WIDE)


def dot_rt(left, right):
    return lax.dot_general(left, right, (((1,), (1,)), ((), ())), preferred_element_type=WIDE)


def dot_lt(left, right):
    return lax.dot_general(left, right, (((0,), (0,)), ((), ())), preferred_element_type=WIDE)


def segments(value, count):
    size = value.shape[1] // count
    return [value[:, i * size : (i + 1) * size] for i in range(count)]


def from_width(value, parts):
    return sum(dot(s, p) for s, p in zip(segments(value, len(parts)), parts))


def to_width(value, parts):
    return jnp.concatenate([dot(value, p) for p in parts], 1)


def from_width_rt(value, parts):
    return sum(dot_rt(s, p) for s, p in zip(segments(value, len(parts)), parts))


def to_width_rt(value, parts):
    return jnp.concatenate([dot_rt(value, p) for p in parts], 1)


def stats(values):
    center = values - jnp.mean(values, -1, keepdims=True)
    return center, lax.rsqrt(jnp.mean(center * center, -1, keepdims=True) + EPS)


def norm_back(xhat, spread, gain, upstream):
    z = upstream * gain
    mean_z = jnp.mean(z, -1, keepdims=True)
    mean_zx = jnp.mean(z * xhat, -1, keepdims=True)
    return (
        spread * (z - mean_z - xhat * mean_zx),
        jnp.sum(upstream * xhat, 0),
        jnp.sum(upstream, 0),
    )


def sum_tensor_rows(value):
    rows = value.shape[0] // 2
    value = pin(value)
    value = value[:rows].astype(WIDE) + swap(value[rows:], "tensor", 1).astype(WIDE)
    bit = 2
    while bit < lax.axis_size("tensor"):
        value = pin(value.astype(LOW))
        value = value.astype(WIDE) + swap(value, "tensor", bit).astype(WIDE)
        bit *= 2
    return value


def gather_rows(piece, size):
    mine = [piece] + [swap(piece, "context", k) for k in range(1, lax.axis_size("context"))]
    rows = piece.shape[0]
    theirs = swap(jnp.concatenate(mine, 0), "tensor", 1)
    blocks = []
    for k, own in enumerate(mine):
        blocks += [own, theirs[k * rows : (k + 1) * rows]]
    return jnp.concatenate([b[:size] for b in blocks], 0), [b[size:] for b in blocks]


def params(limit_mb=48):
    return pltpu.CompilerParams(vmem_limit_bytes=limit_mb << 20)


def pack_kernel(query, key, value, *rest):
    vectors, (qbias, vbias, ebias), out, lines, work = rest[:6], rest[6:9], rest[9], rest[10], rest[11]
    share, columns = query.shape
    for n, ref in enumerate((query, key, value)):
        out[:share, n * columns : (n + 1) * columns] = ref[...]
    work[...] = jnp.zeros_like(work)
    for n, ref in enumerate(vectors):
        work[n : n + 1, :share] = ref[...].reshape(1, share).astype(WIDE)
    mine = lax.axis_index("fsdp")

    def placed(ref, total):
        size = ref.shape[0]
        row = lax.broadcasted_iota(jnp.int32, (size, total), 0)
        column = lax.broadcasted_iota(jnp.int32, (size, total), 1)
        return dot_lt(ref[...], (column == row + mine * size).astype(LOW))

    heads, units = qbias.shape[1], ebias.shape[1]
    ways = lax.axis_size("fsdp")
    work[8 : 8 + heads, 0 : qbias.shape[0] * ways] = placed(qbias, qbias.shape[0] * ways)
    work[8 : 8 + heads, 128 : 128 + vbias.shape[0] * ways] = placed(vbias, vbias.shape[0] * ways)
    work[8 : 8 + units, 256 : 256 + ebias.shape[0] * ways] = placed(ebias, ebias.shape[0] * ways)
    lines[...] = work[...]
    out[share:, :] = work[...].astype(LOW)


def pack(query, key, value, vectors, biases):
    share, columns = query.shape
    return pl.pallas_call(
        pack_kernel,
        out_shape=(
            jax.ShapeDtypeStruct((share + 16, 3 * columns), LOW),
            jax.ShapeDtypeStruct((16, 3 * columns), WIDE),
        ),
        scratch_shapes=[pltpu.VMEM((16, 3 * columns), WIDE)],
        compiler_params=params(),
    )(query, key, value, *vectors, *biases)


def head_mask(shape, head, head_dim):
    lane = lax.broadcasted_iota(jnp.int32, shape, 1)
    return (lane >= head * head_dim) & (lane < (head + 1) * head_dim)


def attend_kernel(heads, head_dim, start, rows, qkv, bias, out):
    features = heads * head_dim
    q = qkv[start : start + rows, :features]
    k = qkv[:, features : 2 * features]
    v = qkv[:, 2 * features :]
    scale = head_dim**-0.5
    total = jnp.zeros((rows, features), WIDE)
    for h in range(heads):
        mine = head_mask(q.shape, h, head_dim)
        scores = dot_rt(jnp.where(mine, q, jnp.zeros_like(q)), k) * scale + bias[...]
        top = jnp.max(scores, -1, keepdims=True)
        raw = jnp.exp(scores - top)
        low = jnp.sum(raw, -1, keepdims=True)
        got = dot(raw.astype(LOW), v) / low
        total = jnp.where(mine, got, total)
    out[...] = total.astype(LOW)


def attend(qkv, bias, heads, head_dim, start, rows):
    features = heads * head_dim
    length = qkv.shape[0]
    return pl.pallas_call(
        lambda *refs: attend_kernel(heads, head_dim, start, rows, *refs),
        out_shape=jax.ShapeDtypeStruct((rows, features), LOW),
        compiler_params=params(),
        cost_estimate=pl.CostEstimate(
            flops=4 * rows * length * features,
            bytes_accessed=qkv.size * 2 + rows * features * 2,
            transcendentals=rows * length * heads,
        ),
    )(qkv, bias)


def attend_back_kernel(heads, head_dim, qkv, bias, grad, out):
    features = heads * head_dim
    q = qkv[:, :features]
    k = qkv[:, features : 2 * features]
    v = qkv[:, 2 * features :]
    g = grad[...]
    scale = head_dim**-0.5
    zero = jnp.zeros_like(q)
    shape = q.shape
    totals = [jnp.zeros(shape, WIDE) for _ in range(3)]
    for h in range(heads):
        mine = head_mask(shape, h, head_dim)
        qm = jnp.where(mine, q, zero)
        gm = jnp.where(mine, g, zero)
        scores = dot_rt(k, qm) * scale + bias[...]
        raw = jnp.exp(scores - jnp.max(scores, 0, keepdims=True))
        weights = raw * (1.0 / jnp.sum(raw, 0, keepdims=True))
        grad_probs = dot_rt(v, gm)
        delta = jnp.sum(weights * grad_probs, 0, keepdims=True)
        grad_scores = (weights * (grad_probs - delta)).astype(LOW)
        totals[0] = jnp.where(mine, dot_lt(grad_scores, k) * scale, totals[0])
        totals[1] = jnp.where(mine, dot(grad_scores, q) * scale, totals[1])
        totals[2] = jnp.where(mine, dot(weights.astype(LOW), g), totals[2])
    for n in range(3):
        out[:, n * features : (n + 1) * features] = totals[n].astype(LOW)


def attend_back(qkv, bias, grad, heads, head_dim):
    length, columns = qkv.shape
    return pl.pallas_call(
        lambda *refs: attend_back_kernel(heads, head_dim, *refs),
        out_shape=jax.ShapeDtypeStruct((length, columns), LOW),
        compiler_params=params(),
        cost_estimate=pl.CostEstimate(
            flops=10 * length * length * heads * head_dim,
            bytes_accessed=qkv.size * 4 + grad.size * 2,
            transcendentals=length * length * heads,
        ),
    )(qkv, bias, grad)


def on_device(
    tokens,
    cotangent,
    valid_count,
    gain_first,
    shift_first,
    query_weight,
    query_bias,
    key_weight,
    value_weight,
    value_bias,
    output_weight,
    output_bias,
    gain_second,
    shift_second,
    expand_weight,
    expand_bias,
    reduce_weight,
    reduce_bias,
):
    images, seq, width = tokens.shape
    ways = lax.axis_size("fsdp")
    pair = ways == 2
    cycle = lax.axis_size("context")
    mine = lax.axis_index("fsdp")
    place = lax.axis_index("context")
    core = lax.axis_index("tensor") & 1
    share = gain_first.shape[0]
    heads = query_bias.shape[1]
    head_dim = query_bias.shape[0] * ways
    features = heads * head_dim
    half = seq // 2
    second = mine == 1

    def turned(value):
        if not pair:
            return value
        low, high = jnp.split(value, 2, -1)
        return jnp.where(second, jnp.concatenate([high, low], -1), value)

    def own_piece(value):
        return turned(lax.dynamic_slice_in_dim(value.reshape(seq, width), core * half, half, 0))

    token_piece = own_piece(tokens)
    cot_piece = own_piece(cotangent)
    vectors = (gain_first, shift_first, output_bias, gain_second, shift_second, reduce_bias)
    biases = (query_bias, value_bias, expand_bias)

    every, _ = gather_rows(token_piece, half)
    if pair:
        message, lines = pack(query_weight, key_weight, value_weight, vectors, biases)
        first = swap(message, "fsdp", 1)
        qkv_parts = (message[:share], first[:share])
        their_lines = first[share:].astype(WIDE)
        gain_one, shift_one, outb, gain_two, shift_two, reduceb = (
            jnp.concatenate([lines[n : n + 1, :share], their_lines[n : n + 1, :share]], 1)
            for n in range(6)
        )
        both = lines[8:] + their_lines[8:]
        qbias = both[:heads, :head_dim].reshape(1, -1)
        vbias = both[:heads, 128 : 128 + head_dim].reshape(1, -1)
        units_each = expand_bias.shape[0] * ways
        ebias = both[: expand_bias.shape[1], 256 : 256 + units_each].reshape(1, -1)
    else:
        gather = lambda v, axis=0: lax.all_gather(v, "fsdp", axis=axis, tiled=True)
        qkv_parts = (gather(jnp.concatenate([query_weight, key_weight, value_weight], 1)),)
        gain_one, shift_one, outb, gain_two, shift_two, reduceb = (
            gather(v).astype(WIDE).reshape(1, -1) for v in vectors
        )
        qbias, vbias, ebias = (gather(v).astype(WIDE).T.reshape(1, -1) for v in biases)

    center, spread = stats(every.astype(WIDE))
    xhat_all = center * spread
    normed_all = (xhat_all * gain_one + shift_one).astype(LOW)
    qkv_bias = jnp.concatenate([qbias, jnp.zeros_like(qbias), vbias], 1)
    qkv = (from_width(normed_all, qkv_parts) + qkv_bias).astype(LOW)
    steps = jnp.arange(half, dtype=jnp.int32)
    positions = jnp.concatenate(
        [(place ^ k) * seq + (core ^ j) * half + steps for k in range(cycle) for j in range(2)]
    )
    bias = jnp.where(positions < valid_count[0], 0.0, -1e30).astype(WIDE)
    context_own = attend(qkv, bias[None, :], heads, head_dim, 0, seq)

    if pair:
        output_parts = (output_weight, swap(after(output_weight, first), "fsdp", 1))
        expand_parts = (expand_weight, swap(after(expand_weight, first), "fsdp", 1))
        reduce_parts = (reduce_weight, swap(after(reduce_weight, context_own), "fsdp", 1))
    else:
        output_parts = (gather(output_weight, 1),)
        expand_parts = (gather(expand_weight),)
        reduce_parts = (gather(reduce_weight, 1),)

    branch = sum_tensor_rows(to_width(context_own, output_parts).astype(LOW)) + outb
    hidden = token_piece.astype(WIDE) + branch
    center_two, spread_two = stats(hidden)
    xhat_two = center_two * spread_two
    normed_piece = (xhat_two * gain_two + shift_two).astype(LOW)

    cot_all, _ = gather_rows(after(cot_piece, every), half)
    normed_two, _ = gather_rows(normed_piece, half)
    expanded = from_width(normed_two, expand_parts) + ebias
    cdf = 0.5 * (1.0 + lax.erf(expanded * (2.0**-0.5)))
    activated = (expanded * cdf).astype(LOW)
    slope = cdf + expanded * jnp.exp(-0.5 * expanded * expanded) * 0.3989422804014327
    grad_expanded = (from_width_rt(cot_all, reduce_parts) * slope).astype(LOW)
    grad_normed_two = sum_tensor_rows(to_width_rt(grad_expanded[:seq], expand_parts).astype(LOW))

    def scatter(value, axis):
        return lax.psum_scatter(value.astype(LOW), "fsdp", scatter_dimension=axis, tiled=True)

    def weight_grad(left, right, along):
        if not pair:
            return scatter(dot_lt(left, right), along).astype(WIDE)
        if along:
            own, other = segments(right, 2)
            away = dot_lt(left, other).astype(LOW)
            return dot_lt(left, own) + swap(away, "fsdp", 1).astype(WIDE)
        own, other = segments(left, 2)
        away = dot_lt(other, right).astype(LOW)
        return dot_lt(own, right) + swap(away, "fsdp", 1).astype(WIDE)

    grad_reduce = weight_grad(activated, cot_all, 1)
    grad_expand = weight_grad(normed_two, grad_expanded, 0)

    upstream = cot_piece.astype(WIDE)
    grad_hidden, gain_two_sum, shift_two_sum = norm_back(
        xhat_two, spread_two, gain_two, grad_normed_two
    )
    grad_hidden = grad_hidden + upstream
    tail = jnp.stack([gain_two_sum, shift_two_sum] + [jnp.zeros_like(gain_two_sum)] * 14)
    grad_branch, tails = gather_rows(
        jnp.concatenate([grad_hidden, tail], 0).astype(LOW), half
    )
    norm_sums = sum(t[:2].astype(WIDE) for t in tails)
    grad_context = from_width_rt(grad_branch, output_parts).astype(LOW)
    grad_qkv = attend_back(qkv, bias[:, None], grad_context, heads, head_dim)

    grad_normed_one = sum_tensor_rows(to_width_rt(grad_qkv[:seq], qkv_parts).astype(LOW))
    center_one, spread_one = stats(token_piece.astype(WIDE))
    grad_inputs, _, _ = norm_back(center_one * spread_one, spread_one, gain_one, grad_normed_one)

    def both_cores(value):
        theirs = swap(value, "tensor", 1)
        upper = core == 1
        return turned(
            jnp.concatenate([jnp.where(upper, theirs, value), jnp.where(upper, value, theirs)], 0)
        ).reshape(tokens.shape)

    grad_tokens = both_cores(grad_inputs + grad_hidden)

    reduced = sum_tensor_rows(
        to_width(after(activated[:seq], grad_branch), reduce_parts).astype(LOW)
    )
    output = both_cores((hidden + reduced + reduceb).astype(LOW))

    def own_rows(value):
        size = value.shape[0] // ways
        return lax.dynamic_slice_in_dim(value, mine * size, size, 0)

    context_rest = attend(
        after(qkv, branch), bias[None, :], heads, head_dim, seq, (cycle - 1) * seq
    )
    context_all = jnp.concatenate([context_own, context_rest], 0)
    sums = jnp.concatenate(
        [
            jnp.sum(grad_branch.astype(WIDE), 0, keepdims=True),
            norm_sums,
            jnp.sum(cot_all.astype(WIDE), 0, keepdims=True),
        ],
        0,
    )
    unit_sum = jnp.sum(grad_expanded.astype(WIDE), 0).reshape(-1, share)
    if pair:
        branch_own, branch_other = segments(grad_branch, 2)
        sums_own, sums_other = segments(sums, 2)
        filler = jnp.zeros((-(features + 4 + unit_sum.shape[0]) % 16, share), WIDE)
        own = jnp.concatenate([dot_lt(context_all, branch_own), sums_own, unit_sum, filler], 0)
        away = jnp.concatenate(
            [dot_lt(context_all, branch_other), sums_other, unit_sum, filler], 0
        )
        own = own + swap(away.astype(LOW), "fsdp", 1).astype(WIDE)
        grad_output, sums, unit_sum = (
            own[:features],
            own[features : features + 4],
            own[features + 4 : features + 4 + unit_sum.shape[0]],
        )
    else:
        grad_output = scatter(dot_lt(context_all, grad_branch), 1).astype(WIDE)
        sums = scatter(sums, 1).astype(WIDE)
        unit_sum = lax.psum(unit_sum, "fsdp")
    grad_ebias = own_rows(unit_sum.reshape(-1, expand_bias.shape[0] * ways).T)

    head_sum = jnp.sum(grad_qkv.astype(WIDE), 0, keepdims=True)
    grad_all = to_width_rt(grad_qkv, qkv_parts)
    first_sums = jnp.stack([jnp.sum(grad_all * xhat_all, 0), jnp.sum(grad_all, 0)])
    if pair:
        columns = 3 * features
        own_side, other_side = segments(first_sums, 2)
        wide = lambda v: jnp.pad(v, ((0, 0), (0, columns - share)))
        filler = jnp.zeros((13, columns), WIDE)
        normed_own, normed_other = segments(normed_all, 2)
        own = jnp.concatenate([dot_lt(normed_own, grad_qkv), head_sum, wide(own_side), filler], 0)
        away = jnp.concatenate(
            [dot_lt(normed_other, grad_qkv), head_sum, wide(other_side), filler], 0
        )
        own = own + swap(away.astype(LOW), "fsdp", 1).astype(WIDE)
        grad_weights, head_sum = own[:share], own[share]
        first_sums = own[share + 1 : share + 3, :share]
    else:
        grad_weights = scatter(dot_lt(normed_all, grad_qkv), 0).astype(WIDE)
        head_sum = lax.psum(head_sum, "fsdp")[0]
        first_sums = scatter(first_sums, 1).astype(WIDE)
    bit = 1
    while bit < lax.axis_size("tensor"):
        first_sums = first_sums + swap(first_sums, "tensor", bit)
        bit *= 2
    grad_query, grad_key, grad_value = (
        grad_weights[:, n * features : (n + 1) * features] for n in range(3)
    )
    grad_qbias, grad_vbias = (
        own_rows(head_sum[n * features : (n + 1) * features].reshape(heads, head_dim).T)
        for n in (0, 2)
    )
    return (
        output,
        grad_tokens,
        first_sums[0],
        first_sums[1],
        grad_query,
        grad_qbias,
        grad_key,
        grad_value,
        grad_vbias,
        grad_output,
        sums[0],
        sums[1],
        sums[2],
        grad_expand,
        grad_ebias,
        grad_reduce,
        sums[3],
    )


def solution(mesh):
    rows = P("fsdp", "context", None)
    vector = P("fsdp")
    split = P("fsdp", "tensor")
    turned = P("tensor", "fsdp")
    in_specs = (rows, rows, vector, vector, vector, split, split, split, split, split)
    in_specs += (turned, vector, vector, vector, split, split, turned, vector)
    out_specs = (rows, rows, vector, vector, split, split, split, split, split)
    out_specs += (turned, vector, vector, vector, split, split, turned, vector)
    return jax.shard_map(
        on_device, mesh=mesh, in_specs=in_specs, out_specs=out_specs, check_vma=False
    )
```

```python
import jax
import jax.numpy as jnp
from jax import lax
from jax.experimental import pallas as pl
from jax.experimental.pallas import tpu as pltpu
from jax.sharding import PartitionSpec as P

EPS = 1e-06
LOW = jnp.bfloat16
WIDE = jnp.float32


def swap(block, axis, bit):
    return lax.ppermute(block, axis, [(i, i ^ bit) for i in range(lax.axis_size(axis))])


def after(value, *others):
    return lax.optimization_barrier((value, *others))[0]


def pin(value):
    return lax.optimization_barrier(value)


def dot(left, right):
    return lax.dot_general(left, right, (((1,), (0,)), ((), ())), preferred_element_type=WIDE)


def dot_rt(left, right):
    return lax.dot_general(left, right, (((1,), (1,)), ((), ())), preferred_element_type=WIDE)


def dot_lt(left, right):
    return lax.dot_general(left, right, (((0,), (0,)), ((), ())), preferred_element_type=WIDE)


def segments(value, count):
    size = value.shape[1] // count
    return [value[:, i * size : (i + 1) * size] for i in range(count)]


def from_width(value, parts):
    return sum(dot(s, p) for s, p in zip(segments(value, len(parts)), parts))


def to_width(value, parts):
    return jnp.concatenate([dot(value, p) for p in parts], 1)


def from_width_rt(value, parts):
    return sum(dot_rt(s, p) for s, p in zip(segments(value, len(parts)), parts))


def to_width_rt(value, parts):
    return jnp.concatenate([dot_rt(value, p) for p in parts], 1)


def sum_cores(keep, send):
    return (keep.astype(WIDE) + swap(send, "tensor", 1).astype(WIDE)).astype(LOW)


def last_terms(keep, send):
    value = pin(sum_cores(keep, send))
    bit = 2
    while True:
        got = swap(value, "tensor", bit)
        bit *= 2
        if bit >= lax.axis_size("tensor"):
            return value, got
        value = pin((value.astype(WIDE) + got.astype(WIDE)).astype(LOW))


def spread_context(piece):
    return [piece] + [swap(piece, "context", k) for k in range(1, lax.axis_size("context"))]


def woven(mine, theirs):
    return [block for both in zip(mine, theirs) for block in both]


def gather_pieces(piece):
    mine = spread_context(piece)
    return woven(mine, [swap(m, "tensor", 1) for m in mine])


def kernel(body, out_shape, *args, flops=0, moved=0, scratch=(), in_specs=None):
    extra = {} if in_specs is None else {"in_specs": in_specs}
    return pl.pallas_call(
        body,
        out_shape=out_shape,
        scratch_shapes=list(scratch),
        compiler_params=pltpu.CompilerParams(vmem_limit_bytes=48 << 20),
        cost_estimate=pl.CostEstimate(flops=flops, bytes_accessed=moved, transcendentals=0),
        **extra,
    )(*args)


def low(*shape):
    return jax.ShapeDtypeStruct(shape, LOW)


def wide(*shape):
    return jax.ShapeDtypeStruct(shape, WIDE)


QBIAS, VBIAS, EBIAS = 6, 7, 8


def pack_body(*refs):
    sources, (lines, message), copies = refs[:9], refs[9:11], refs[11:20]
    arrived = refs[20]
    moves = [
        pltpu.make_async_copy(s, c, arrived.at[n]) for n, (s, c) in enumerate(zip(sources, copies))
    ]
    for m in moves:
        m.start()
    lines[...] = jnp.zeros_like(lines)
    for m in moves:
        m.wait()
    ways = lax.axis_size("fsdp")
    mine = lax.axis_index("fsdp")
    for n, ref in enumerate(copies[:6]):
        lines[n : n + 1, : ref.shape[0]] = ref[...].reshape(1, -1).astype(WIDE)
    for n, ref in zip((QBIAS, VBIAS, EBIAS), copies[6:]):
        groups, size = ref.shape
        each = size * ways
        row = lax.broadcasted_iota(jnp.int32, (size, groups * each), 0)
        column = lax.broadcasted_iota(jnp.int32, (size, groups * each), 1)
        within = column
        for g in range(1, groups):
            within = jnp.where(column >= g * each, column - g * each, within)
        tiled = dot(ref[...], (within == row + mine * size).astype(LOW))
        group = lax.broadcasted_iota(jnp.int32, tiled.shape, 0)
        column = lax.broadcasted_iota(jnp.int32, tiled.shape, 1)
        keep = (column >= group * each) & (column < (group + 1) * each)
        lines[n : n + 1, : groups * each] = jnp.sum(
            jnp.where(keep, tiled, 0.0), 0, keepdims=True
        )
    message[...] = lines[...].astype(LOW)


def merge_body(own, got, out):
    share = own.shape[1] // 2
    theirs = got[...].astype(WIDE)
    out[...] = own[...] + theirs
    out[:QBIAS, :share] = own[:QBIAS, :share]
    out[:QBIAS, share:] = theirs[:QBIAS, :share]


def normed_rows(values):
    center = values - jnp.mean(values, -1, keepdims=True)
    return center * lax.rsqrt(jnp.mean(center * center, -1, keepdims=True) + EPS)


def norm_back_rows(values, gain, upstream):
    center = values - jnp.mean(values, -1, keepdims=True)
    spread = lax.rsqrt(jnp.mean(center * center, -1, keepdims=True) + EPS)
    xhat = center * spread
    z = upstream * gain
    grad = spread * (
        z - jnp.mean(z, -1, keepdims=True) - xhat * jnp.mean(z * xhat, -1, keepdims=True)
    )
    return grad, xhat


def head_mask(shape, head, head_dim):
    lane = lax.broadcasted_iota(jnp.int32, shape, 1)
    return (lane >= head * head_dim) & (lane < (head + 1) * head_dim)


def attend_rows(heads, head_dim, start, rows, qkv, bias):
    features = heads * head_dim
    q = qkv[start : start + rows, :features]
    k = qkv[:, features : 2 * features]
    v = qkv[:, 2 * features :]
    scale = head_dim**-0.5
    total = jnp.zeros((rows, features), WIDE)
    for h in range(heads):
        mine = head_mask(q.shape, h, head_dim)
        scores = dot_rt(jnp.where(mine, q, jnp.zeros_like(q)), k) * scale + bias[...]
        raw = jnp.exp(scores - jnp.max(scores, -1, keepdims=True))
        got = dot(raw.astype(LOW), v) / jnp.sum(raw, -1, keepdims=True)
        total = jnp.where(mine, got, total)
    return total.astype(LOW)


def first_body(heads, head_dim, blocks, ways, *refs):
    pieces, refs = refs[:blocks], refs[blocks:]
    vec, bias = refs[:2]
    weights = [refs[2 + n * ways : 2 + (n + 1) * ways] for n in range(3)]
    outs = refs[2 + 3 * ways : 2 + 4 * ways]
    xhat, normed, qkv, context, keep, send = refs[2 + 4 * ways :]
    rows = pieces[0].shape[0]
    features = heads * head_dim
    for n, piece in enumerate(pieces):
        part = normed_rows(piece[...].astype(WIDE))
        xhat[n * rows : (n + 1) * rows, :] = part.astype(LOW)
        normed[n * rows : (n + 1) * rows, :] = (part * vec[0:1, :] + vec[1:2, :]).astype(LOW)
    size = normed.shape[1] // ways
    for n, row in enumerate((QBIAS, None, VBIAS)):
        got = sum(
            dot(normed[:, i * size : (i + 1) * size], w[...]) for i, w in enumerate(weights[n])
        )
        if row is not None:
            got = got + vec[row : row + 1, :features]
        qkv[:, n * features : (n + 1) * features] = got.astype(LOW)
    context[...] = attend_rows(heads, head_dim, 0, 2 * rows, qkv, bias)
    for i, w in enumerate(outs):
        part = dot(context[...], w[...]).astype(LOW)
        keep[:, i * size : (i + 1) * size] = part[:rows]
        send[:, i * size : (i + 1) * size] = part[rows:]


def rest_body(heads, head_dim, start, qkv, bias, out):
    out[...] = attend_rows(heads, head_dim, start, out.shape[0], qkv, bias)


def second_body(tokens, near, far, vec, hidden, normed):
    total = tokens[...].astype(WIDE) + (near[...].astype(WIDE) + far[...].astype(WIDE))
    total = total + vec[2:3, :]
    hidden[...] = total
    normed[...] = (normed_rows(total) * vec[3:4, :] + vec[4:5, :]).astype(LOW)


def second_back_body(near, far, hidden, cot, vec, grad_hidden, grad_branch, sums):
    upstream = near[...].astype(WIDE) + far[...].astype(WIDE)
    grad, xhat = norm_back_rows(hidden[...], vec[3:4, :], upstream)
    total = grad + cot[...].astype(WIDE)
    grad_hidden[...] = total
    grad_branch[...] = total.astype(LOW)
    sums[...] = jnp.zeros_like(sums)
    sums[0:1, :] = jnp.sum(upstream * xhat, 0, keepdims=True)
    sums[1:2, :] = jnp.sum(upstream, 0, keepdims=True)


def attend_back_body(heads, head_dim, blocks, ways, *refs):
    pieces, refs = refs[:blocks], refs[blocks:]
    qkv, bias = refs[:2]
    outs = refs[2 : 2 + ways]
    weights = [refs[2 + (n + 1) * ways : 2 + (n + 2) * ways] for n in range(3)]
    branch, grad_qkv, keep, send, sums, head_sums = refs[2 + 4 * ways :]
    rows = pieces[0].shape[0]
    features = heads * head_dim
    for n, piece in enumerate(pieces):
        branch[n * rows : (n + 1) * rows, :] = piece[...]
    size = branch.shape[1] // ways
    g = sum(
        dot_rt(branch[:, i * size : (i + 1) * size], w[...]) for i, w in enumerate(outs)
    ).astype(LOW)
    q = qkv[:, :features]
    k = qkv[:, features : 2 * features]
    v = qkv[:, 2 * features :]
    scale = head_dim**-0.5
    zero = jnp.zeros_like(q)
    totals = [jnp.zeros(q.shape, WIDE) for _ in range(3)]
    for h in range(heads):
        mine = head_mask(q.shape, h, head_dim)
        scores = dot_rt(k, jnp.where(mine, q, zero)) * scale + bias[...]
        raw = jnp.exp(scores - jnp.max(scores, 0, keepdims=True))
        probs = raw * (1.0 / jnp.sum(raw, 0, keepdims=True))
        grad_probs = dot_rt(v, jnp.where(mine, g, zero))
        delta = jnp.sum(probs * grad_probs, 0, keepdims=True)
        grad_scores = (probs * (grad_probs - delta)).astype(LOW)
        totals[0] = jnp.where(mine, dot_lt(grad_scores, k) * scale, totals[0])
        totals[1] = jnp.where(mine, dot(grad_scores, q) * scale, totals[1])
        totals[2] = jnp.where(mine, dot(probs.astype(LOW), g), totals[2])
    head_sums[...] = jnp.zeros_like(head_sums)
    for n in range(3):
        part = totals[n].astype(LOW)
        grad_qkv[:, n * features : (n + 1) * features] = part
        head_sums[0:1, n * features : (n + 1) * features] = jnp.sum(
            part.astype(WIDE), 0, keepdims=True
        )
    for i in range(ways):
        part = sum(
            dot_rt(grad_qkv[: 2 * rows, n * features : (n + 1) * features], weights[n][i][...])
            for n in range(3)
        ).astype(LOW)
        keep[:, i * size : (i + 1) * size] = part[:rows]
        send[:, i * size : (i + 1) * size] = part[rows:]
    sums[...] = jnp.zeros_like(sums)
    sums[0:1, :] = jnp.sum(branch[...].astype(WIDE), 0, keepdims=True)


def first_sums_body(ways, grad_qkv, xhat, *refs):
    weights = [refs[n * ways : (n + 1) * ways] for n in range(3)]
    out = refs[3 * ways]
    features = grad_qkv.shape[1] // 3
    size = xhat.shape[1] // ways
    out[...] = jnp.zeros_like(out)
    for i in range(ways):
        part = sum(
            dot_rt(grad_qkv[:, n * features : (n + 1) * features], weights[n][i][...])
            for n in range(3)
        )
        columns = slice(i * size, (i + 1) * size)
        out[0:1, columns] = jnp.sum(part * xhat[:, columns].astype(WIDE), 0, keepdims=True)
        out[1:2, columns] = jnp.sum(part, 0, keepdims=True)


def first_back_body(near, far, tokens, grad_hidden, vec, out):
    upstream = near[...].astype(WIDE) + far[...].astype(WIDE)
    grad, _ = norm_back_rows(tokens[...].astype(WIDE), vec[0:1, :], upstream)
    out[...] = grad + grad_hidden[...]


def on_device(
    tokens,
    cotangent,
    valid_count,
    gain_first,
    shift_first,
    query_weight,
    query_bias,
    key_weight,
    value_weight,
    value_bias,
    output_weight,
    output_bias,
    gain_second,
    shift_second,
    expand_weight,
    expand_bias,
    reduce_weight,
    reduce_bias,
):
    images, seq, width = tokens.shape
    ways = lax.axis_size("fsdp")
    pair = ways == 2
    parts = 2 if pair else 1
    cycle = lax.axis_size("context")
    mine = lax.axis_index("fsdp")
    place = lax.axis_index("context")
    core = lax.axis_index("tensor") & 1
    share = gain_first.shape[0]
    heads = query_bias.shape[1]
    head_dim = query_bias.shape[0] * ways
    features = heads * head_dim
    units = expand_weight.shape[1]
    half = seq // 2
    blocks = 2 * cycle
    length = cycle * seq
    second = mine == 1

    def turned(value):
        if not pair:
            return value
        left, right = jnp.split(value, 2, -1)
        return jnp.where(second, jnp.concatenate([right, left], -1), value)

    def piece_of(value, which):
        return turned(lax.dynamic_slice_in_dim(value.reshape(seq, width), which * half, half, 0))

    token_piece = piece_of(tokens, core)
    mine_tokens = spread_context(token_piece)
    token_pieces = woven(
        mine_tokens,
        [piece_of(tokens, 1 - core)] + [swap(m, "tensor", 1) for m in mine_tokens[1:]],
    )
    vectors = (gain_first, shift_first, output_bias, gain_second, shift_second, reduce_bias)
    biases = (query_bias, value_bias, expand_bias)
    thirds = (query_weight, key_weight, value_weight)

    if pair:
        across = lambda v: swap(v, "fsdp", 1)
        qkv_parts = [(w, across(w)) for w in thirds]
        lines, message = kernel(
            pack_body,
            (wide(16, width), low(16, width)),
            *vectors,
            *(b.T for b in biases),
            in_specs=[pl.BlockSpec(memory_space=pl.ANY)] * 9,
            scratch=[pltpu.VMEM(v.shape, LOW) for v in vectors]
            + [pltpu.VMEM(b.shape[::-1], LOW) for b in biases]
            + [pltpu.SemaphoreType.DMA((9,))],
        )
        vec = kernel(merge_body, wide(16, width), lines, across(message))
        output_parts = (output_weight, across(output_weight))
    else:
        gather = lambda v, axis=0: lax.all_gather(v, "fsdp", axis=axis, tiled=True)
        qkv_parts = [(gather(w),) for w in thirds]
        rows = [gather(v).reshape(1, -1) for v in vectors]
        rows += [gather(b).T.reshape(1, -1) for b in biases]
        vec = jnp.concatenate(
            [jnp.pad(r, ((0, 0), (0, width - r.shape[1]))) for r in rows]
            + [jnp.zeros((16 - len(rows), width), LOW)],
            0,
        ).astype(WIDE)
        output_parts = (gather(output_weight, 1),)
    flat_qkv = [w for group in qkv_parts for w in group]

    steps = jnp.arange(half, dtype=jnp.int32)
    positions = jnp.concatenate(
        [(place ^ k) * seq + (core ^ j) * half + steps for k in range(cycle) for j in range(2)]
    )
    bias = jnp.where(positions < valid_count[0], 0.0, -1e30).astype(WIDE)
    xhat_all, normed_all, qkv, context_own, keep, send = kernel(
        lambda *refs: first_body(heads, head_dim, blocks, parts, *refs),
        (
            low(length, width),
            low(length, width),
            low(length, 3 * features),
            low(seq, features),
            low(half, width),
            low(half, width),
        ),
        *token_pieces,
        vec,
        bias[None, :],
        *flat_qkv,
        *output_parts,
        flops=6 * length * width * features,
        moved=10 * length * width,
    )

    if pair:
        expand_parts = (expand_weight, across(after(expand_weight, flat_qkv[-1])))
        reduce_parts = (reduce_weight, across(after(reduce_weight, keep)))
    else:
        expand_parts = (gather(expand_weight),)
        reduce_parts = (gather(reduce_weight, 1),)

    near, far = last_terms(keep, send)
    hidden, normed_piece = kernel(
        second_body, (wide(half, width), low(half, width)), token_piece, near, far, vec
    )

    cot_piece = piece_of(cotangent, core)
    cot_all = jnp.concatenate(gather_pieces(after(cot_piece, mine_tokens[-1])), 0)
    normed_two = jnp.concatenate(gather_pieces(normed_piece), 0)
    expanded = from_width(normed_two, expand_parts) + vec[EBIAS : EBIAS + 1, :units]
    cdf = 0.5 * (1.0 + lax.erf(expanded * (2.0**-0.5)))
    activated = (expanded * cdf).astype(LOW)
    slope = cdf + expanded * jnp.exp(-0.5 * expanded * expanded) * 0.3989422804014327
    grad_expanded = (from_width_rt(cot_all, reduce_parts) * slope).astype(LOW)
    near, far = last_terms(
        to_width_rt(grad_expanded[:half], expand_parts).astype(LOW),
        to_width_rt(grad_expanded[half:seq], expand_parts).astype(LOW),
    )
    grad_hidden, grad_piece, norm_sums = kernel(
        second_back_body,
        (wide(half, width), low(half, width), wide(8, width)),
        near,
        far,
        hidden,
        cot_piece,
        vec,
    )

    def scatter(value, axis):
        return lax.psum_scatter(value.astype(LOW), "fsdp", scatter_dimension=axis, tiled=True)

    def weight_grad(left, right, along):
        if not pair:
            return scatter(dot_lt(left, right), along).astype(WIDE)
        if along:
            own, other = segments(right, 2)
            away = across(dot_lt(left, other).astype(LOW))
            return pin(dot_lt(left, own)) + away.astype(WIDE)
        own, other = segments(left, 2)
        away = across(dot_lt(other, right).astype(LOW))
        return pin(dot_lt(own, right)) + away.astype(WIDE)

    grad_reduce = weight_grad(activated, cot_all, 1)
    grad_expand = weight_grad(normed_two, grad_expanded, 0)

    grad_branch, grad_qkv, keep, send, branch_sum, head_sum = kernel(
        lambda *refs: attend_back_body(heads, head_dim, blocks, parts, *refs),
        (
            low(length, width),
            low(length, 3 * features),
            low(half, width),
            low(half, width),
            wide(8, width),
            wide(8, 3 * features),
        ),
        *gather_pieces(grad_piece),
        qkv,
        bias[:, None],
        *output_parts,
        *flat_qkv,
        flops=10 * length * length * features,
        moved=8 * length * width,
    )
    near, far = last_terms(keep, send)
    grad_token_piece = kernel(
        first_back_body, wide(half, width), near, far, token_piece, grad_hidden, vec
    )

    def both_cores(value):
        theirs = swap(value, "tensor", 1)
        upper = core == 1
        return turned(
            jnp.concatenate([jnp.where(upper, theirs, value), jnp.where(upper, value, theirs)], 0)
        ).reshape(tokens.shape)

    grad_tokens = both_cores(grad_token_piece)

    normed_sides = segments(normed_all, parts)
    if pair:
        away = across(dot_lt(normed_sides[1], grad_qkv).astype(LOW))
        grad_weights = pin(dot_lt(normed_sides[0], grad_qkv)) + away.astype(WIDE)
    else:
        grad_weights = scatter(dot_lt(normed_all, grad_qkv), 0).astype(WIDE)
    grad_query, grad_key, grad_value = (
        grad_weights[:, n * features : (n + 1) * features] for n in range(3)
    )

    near, far = last_terms(
        to_width(after(activated[:half], grad_piece), reduce_parts).astype(LOW),
        to_width(after(activated[half:seq], grad_piece), reduce_parts).astype(LOW),
    )
    reduced = near.astype(WIDE) + far.astype(WIDE) + vec[5:6, :]
    output = both_cores((hidden + reduced).astype(LOW))

    def own_rows(value):
        size = value.shape[0] // ways
        return lax.dynamic_slice_in_dim(value, mine * size, size, 0)

    context_rest = kernel(
        lambda *refs: rest_body(heads, head_dim, seq, *refs),
        low(length - seq, features),
        after(qkv, near),
        bias[None, :],
    )
    context_all = jnp.concatenate([context_own, context_rest], 0)
    grad_output = weight_grad(context_all, grad_branch, 1)

    first_sums = kernel(
        lambda *refs: first_sums_body(parts, *refs), wide(8, width), grad_qkv, xhat_all, *flat_qkv
    )[:2]
    bit = 1
    while bit < lax.axis_size("tensor"):
        first_sums = first_sums + swap(first_sums, "tensor", bit)
        bit *= 2
    norm_sums = norm_sums[:2] + swap(norm_sums[:2], "tensor", 1)
    bit = 1
    while bit < cycle:
        norm_sums = norm_sums + swap(norm_sums, "context", bit)
        bit *= 2
    cot_sum = jnp.sum(cot_all.astype(WIDE), 0, keepdims=True)
    unit_sum = jnp.sum(grad_expanded.astype(WIDE), 0, keepdims=True)
    sums = jnp.concatenate([first_sums, norm_sums, branch_sum[:1], cot_sum], 0)
    plain = jnp.concatenate(
        [jnp.pad(head_sum[:1], ((0, 0), (0, width - 3 * features))), unit_sum], 0
    )
    if pair:
        own, other = segments(sums, 2)
        got = across(jnp.concatenate([other, *segments(plain, 2)], 0))
        sums = own + got[:6]
        plain = plain + jnp.concatenate([got[6:8], got[8:10]], 1)
    else:
        sums = scatter(sums, 1).astype(WIDE)
        plain = lax.psum(plain, "fsdp")
    grad_ebias = own_rows(plain[1].reshape(-1, expand_bias.shape[0] * ways).T)
    grad_qbias, grad_vbias = (
        own_rows(plain[0, n * features : (n + 1) * features].reshape(heads, head_dim).T)
        for n in (0, 2)
    )
    return (
        output,
        grad_tokens,
        sums[0],
        sums[1],
        grad_query,
        grad_qbias,
        grad_key,
        grad_value,
        grad_vbias,
        grad_output,
        sums[4],
        sums[2],
        sums[3],
        grad_expand,
        grad_ebias,
        grad_reduce,
        sums[5],
    )


def solution(mesh):
    rows = P("fsdp", "context", None)
    vector = P("fsdp")
    split = P("fsdp", "tensor")
    turned = P("tensor", "fsdp")
    in_specs = (rows, rows, vector, vector, vector, split, split, split, split, split)
    in_specs += (turned, vector, vector, vector, split, split, turned, vector)
    out_specs = (rows, rows, vector, vector, split, split, split, split, split)
    out_specs += (turned, vector, vector, vector, split, split, turned, vector)
    return jax.shard_map(
        on_device, mesh=mesh, in_specs=in_specs, out_specs=out_specs, check_vma=False
    )
```

```python
import jax
import jax.numpy as jnp
from jax import lax
from jax.experimental import pallas as pl
from jax.experimental.pallas import tpu as pltpu
from jax.sharding import PartitionSpec as P

EPS = 1e-06
LOW = jnp.bfloat16
WIDE = jnp.float32


def swap(block, axis, bit):
    return lax.ppermute(block, axis, [(i, i ^ bit) for i in range(lax.axis_size(axis))])


def after(value, *others):
    return lax.optimization_barrier((value, *others))[0]


def pin(value):
    return lax.optimization_barrier(value)


def dot(left, right):
    return lax.dot_general(left, right, (((1,), (0,)), ((), ())), preferred_element_type=WIDE)


def dot_rt(left, right):
    return lax.dot_general(left, right, (((1,), (1,)), ((), ())), preferred_element_type=WIDE)


def dot_lt(left, right):
    return lax.dot_general(left, right, (((0,), (0,)), ((), ())), preferred_element_type=WIDE)


def segments(value, count):
    size = value.shape[1] // count
    return [value[:, i * size : (i + 1) * size] for i in range(count)]


def sum_cores(keep, send):
    return (keep.astype(WIDE) + swap(send, "tensor", 1).astype(WIDE)).astype(LOW)


def last_terms(keep, send):
    value = pin(sum_cores(keep, send))
    bit = 2
    while True:
        got = swap(value, "tensor", bit)
        bit *= 2
        if bit >= lax.axis_size("tensor"):
            return value, got
        value = pin((value.astype(WIDE) + got.astype(WIDE)).astype(LOW))


def spread_context(piece):
    return [piece] + [swap(piece, "context", k) for k in range(1, lax.axis_size("context"))]


def woven(mine, theirs):
    return [block for both in zip(mine, theirs) for block in both]


class Late:
    def __init__(self, ref, copy):
        self.ref, self.copy, self.shape = ref, copy, ref.shape

    def wait(self):
        if self.copy is not None:
            self.copy.wait()
            self.copy = None

    def __getitem__(self, index):
        self.wait()
        return self.ref[index]


def kernel(body, out_shape, *args, count=None, flops=0, moved=0, staged=False, limit=48):
    scalars = [] if count is None else [count]
    first, last = len(scalars), len(scalars) + len(args)

    def run(*refs):
        buffers, arrived = refs[-len(args) - 1 : -1], refs[-1]
        inputs = []
        for n, (source, buffer) in enumerate(zip(refs[first:last], buffers)):
            copy = pltpu.make_async_copy(source, buffer, arrived.at[n])
            copy.start()
            inputs.append(Late(buffer, copy))
        body(*refs[:first], *inputs, *refs[last : -len(args) - 1])
        for late in inputs:
            late.wait()

    scratch = [pltpu.VMEM(a.shape, a.dtype) for a in args] + [pltpu.SemaphoreType.DMA((len(args),))]
    space = pltpu.HBM if staged else pltpu.VMEM
    return pl.pallas_call(
        run if staged else body,
        out_shape=out_shape,
        in_specs=[pl.BlockSpec(memory_space=pltpu.SMEM)] * first
        + [pl.BlockSpec(memory_space=space)] * len(args),
        scratch_shapes=scratch if staged else (),
        compiler_params=pltpu.CompilerParams(vmem_limit_bytes=limit << 20),
        cost_estimate=pl.CostEstimate(flops=flops, bytes_accessed=moved, transcendentals=0),
    )(*scalars, *args)


def low(*shape):
    return jax.ShapeDtypeStruct(shape, LOW)


def wide(*shape):
    return jax.ShapeDtypeStruct(shape, WIDE)


QBIAS, VBIAS, EBIAS = 6, 7, 8


def pack_body(*refs):
    weights, vectors, biases = refs[:3], refs[3:9], refs[9:12]
    message, lines = refs[12:]
    ways = lax.axis_size("fsdp")
    mine = lax.axis_index("fsdp")
    share, columns = weights[0].shape
    lines[...] = jnp.zeros_like(lines)
    for n, ref in enumerate(vectors):
        lines[n : n + 1, :share] = ref[...].reshape(1, -1).astype(WIDE)
    for n, ref in zip((QBIAS, VBIAS, EBIAS), biases):
        groups, size = ref.shape
        each = size * ways
        row = lax.broadcasted_iota(jnp.int32, (size, groups * each), 0)
        column = lax.broadcasted_iota(jnp.int32, (size, groups * each), 1)
        within = column
        for g in range(1, groups):
            within = jnp.where(column >= g * each, column - g * each, within)
        tiled = dot(ref[...], (within == row + mine * size).astype(LOW))
        group = lax.broadcasted_iota(jnp.int32, tiled.shape, 0)
        column = lax.broadcasted_iota(jnp.int32, tiled.shape, 1)
        keep = (column >= group * each) & (column < (group + 1) * each)
        flat = jnp.sum(jnp.where(keep, tiled, 0.0), 0, keepdims=True)
        for at in range(0, groups * each, share):
            part = flat[:, at : at + share]
            lines[n + at // share : n + at // share + 1, : part.shape[1]] = part
    message[share:, :] = lines[...].astype(LOW)
    for n, w in enumerate(weights):
        message[:share, n * columns : (n + 1) * columns] = w[...]


def merge(own, got, out):
    share = out.shape[1] // 2
    out[...] = jnp.zeros_like(out)
    mine, theirs = own[...], got[got.shape[0] - own.shape[0] :, :].astype(WIDE)
    out[:QBIAS, :share] = mine[:QBIAS, :share]
    out[:QBIAS, share:] = theirs[:QBIAS, :share]
    both = mine + theirs
    out[QBIAS : EBIAS + 1, :share] = both[QBIAS : EBIAS + 1, :share]
    out[EBIAS : EBIAS + 1, share:] = both[EBIAS + 1 : EBIAS + 2, :share]


def normed_rows(values):
    center = values - jnp.mean(values, -1, keepdims=True)
    return center * lax.rsqrt(jnp.mean(center * center, -1, keepdims=True) + EPS)


def norm_back_rows(values, gain, upstream):
    center = values - jnp.mean(values, -1, keepdims=True)
    spread = lax.rsqrt(jnp.mean(center * center, -1, keepdims=True) + EPS)
    xhat = center * spread
    z = upstream * gain
    grad = spread * (
        z - jnp.mean(z, -1, keepdims=True) - xhat * jnp.mean(z * xhat, -1, keepdims=True)
    )
    return grad, xhat


def third_of(message, n, size, features):
    return message[:size, n * features : (n + 1) * features]


def key_bias(count, shape, axis, seq):
    step = lax.broadcasted_iota(jnp.int32, shape, axis)
    place = lax.axis_index("context")
    core = lax.axis_index("tensor") & 1
    half = seq // 2
    position = step
    for b in range(shape[axis] // half):
        start = (place ^ (b // 2)) * seq + (core ^ (b % 2)) * half
        position = jnp.where(step >= b * half, step + (start - b * half), position)
    return jnp.where(position < count[0], 0.0, -1e30).astype(WIDE)


def head_mask(shape, head, head_dim):
    lane = lax.broadcasted_iota(jnp.int32, shape, 1)
    return (lane >= head * head_dim) & (lane < (head + 1) * head_dim)


def attend_rows(heads, head_dim, start, rows, qkv, bias):
    features = heads * head_dim
    q = qkv[start : start + rows, :features]
    k = qkv[:, features : 2 * features]
    v = qkv[:, 2 * features :]
    scale = head_dim**-0.5
    total = jnp.zeros((rows, features), WIDE)
    for h in range(heads):
        mine = head_mask(q.shape, h, head_dim)
        scores = dot_rt(jnp.where(mine, q, jnp.zeros_like(q)), k) * scale + bias
        raw = jnp.exp(scores - jnp.max(scores, -1, keepdims=True))
        got = dot(raw.astype(LOW), v) / jnp.sum(raw, -1, keepdims=True)
        total = jnp.where(mine, got, total)
    return total.astype(LOW)


def first_body(heads, head_dim, blocks, ways, count, *refs):
    pieces, refs = refs[:blocks], refs[blocks:]
    packed, lines, refs = refs[:ways], refs[ways], refs[ways + 1 :]
    vec, xhat, normed, qkv, context = refs
    rows = pieces[0].shape[0]
    if ways == 2:
        merge(lines, packed[1], vec)
    else:
        vec[...] = lines[...]
    features = heads * head_dim
    for n, piece in enumerate(pieces):
        part = normed_rows(piece[...].astype(WIDE))
        xhat[n * rows : (n + 1) * rows, :] = part.astype(LOW)
        normed[n * rows : (n + 1) * rows, :] = (part * vec[0:1, :] + vec[1:2, :]).astype(LOW)
    size = normed.shape[1] // ways
    for n, row in enumerate((QBIAS, None, VBIAS)):
        got = sum(
            dot(normed[:, i * size : (i + 1) * size], third_of(w, n, size, features))
            for i, w in enumerate(packed)
        )
        if row is not None:
            got = got + vec[row : row + 1, :features]
        qkv[:, n * features : (n + 1) * features] = got.astype(LOW)
    bias = key_bias(count, (1, blocks * rows), 1, 2 * rows)
    context[...] = attend_rows(heads, head_dim, 0, 2 * rows, qkv, bias)


def out_body(ways, *refs):
    context, weights, (keep, send) = refs[0], refs[1 : 1 + ways], refs[1 + ways :]
    rows, size = keep.shape[0], keep.shape[1] // ways
    for i, w in enumerate(weights):
        part = dot(context[...], w[...]).astype(LOW)
        keep[:, i * size : (i + 1) * size] = part[:rows]
        send[:, i * size : (i + 1) * size] = part[rows:]


def rest_body(heads, head_dim, start, count, qkv, out):
    bias = key_bias(count, (1, qkv.shape[0]), 1, start)
    out[...] = attend_rows(heads, head_dim, start, out.shape[0], qkv, bias)


def second_body(tokens, near, far, vec, hidden, normed):
    total = tokens[...].astype(WIDE) + (near[...].astype(WIDE) + far[...].astype(WIDE))
    total = total + vec[2:3, :]
    hidden[...] = total
    normed[...] = (normed_rows(total) * vec[3:4, :] + vec[4:5, :]).astype(LOW)


def forward_body(blocks, ways, *refs):
    normed, cots, refs = refs[:blocks], refs[blocks : 2 * blocks], refs[2 * blocks :]
    vec, expand, reduce = refs[0], refs[1 : 1 + ways], refs[1 + ways : 1 + 2 * ways]
    normed_all, cot_all, act, grad, keep, send, out_keep, out_send, unit_sum, cot_sum = refs[
        1 + 2 * ways :
    ]
    rows = normed[0].shape[0]
    size = normed_all.shape[1] // ways
    units = act.shape[1]
    total = jnp.zeros((1, normed_all.shape[1]), WIDE)
    for n in range(blocks):
        normed_all[n * rows : (n + 1) * rows, :] = normed[n][...]
        cot_all[n * rows : (n + 1) * rows, :] = cots[n][...]
        total = total + jnp.sum(cots[n][...].astype(WIDE), 0, keepdims=True)
    cot_sum[...] = total
    step = min(256, units, size)
    back = [jnp.zeros((2 * rows, size), WIDE) for _ in range(ways)]
    out = [jnp.zeros((2 * rows, size), WIDE) for _ in range(ways)]
    for at in range(0, units, step):
        columns = slice(at, at + step)
        expands = [w[:, columns] for w in expand]
        reduces = [w[columns, :] for w in reduce]
        sides = [slice(i * size, (i + 1) * size) for i in range(ways)]
        value = sum(dot(normed_all[:, c], w) for c, w in zip(sides, expands))
        value = value + vec[EBIAS : EBIAS + 1, columns]
        cdf = 0.5 * (1.0 + lax.erf(value * (2.0**-0.5)))
        act[:, columns] = (value * cdf).astype(LOW)
        slope = cdf + value * jnp.exp(-0.5 * value * value) * 0.3989422804014327
        part = sum(dot_rt(cot_all[:, c], w) for c, w in zip(sides, reduces))
        part = (part * slope).astype(LOW)
        grad[:, columns] = part
        unit_sum[0:1, columns] = jnp.sum(part.astype(WIDE), 0, keepdims=True)
        own = act[: 2 * rows, columns]
        for i in range(ways):
            back[i] = back[i] + dot_rt(part[: 2 * rows], expands[i])
            out[i] = out[i] + dot(own, reduces[i])
    for i, c in enumerate(sides):
        keep[:, c] = back[i][:rows].astype(LOW)
        send[:, c] = back[i][rows:].astype(LOW)
        out_keep[:, c] = out[i][:rows].astype(LOW)
        out_send[:, c] = out[i][rows:].astype(LOW)


def second_back_body(near, far, hidden, cot, vec, grad_hidden, grad_branch, sums):
    upstream = near[...].astype(WIDE) + far[...].astype(WIDE)
    grad, xhat = norm_back_rows(hidden[...], vec[3:4, :], upstream)
    total = grad + cot[...].astype(WIDE)
    grad_hidden[...] = total
    grad_branch[...] = total.astype(LOW)
    sums[0:1, :] = jnp.sum(upstream * xhat, 0, keepdims=True)
    sums[1:2, :] = jnp.sum(upstream, 0, keepdims=True)


def attend_back_body(heads, head_dim, blocks, ways, count, *refs):
    pieces, refs = refs[:blocks], refs[blocks:]
    outs, qkv, packed = refs[:ways], refs[ways], refs[ways + 1 : 2 * ways + 1]
    normed = refs[2 * ways + 1]
    branch, grad_qkv, keep, send, sums, head_sums, away = refs[2 * ways + 2 :]
    rows = pieces[0].shape[0]
    features = heads * head_dim
    for n, piece in enumerate(pieces):
        branch[n * rows : (n + 1) * rows, :] = piece[...]
    size = branch.shape[1] // ways
    g = sum(
        dot_rt(branch[:, i * size : (i + 1) * size], w[...]) for i, w in enumerate(outs)
    ).astype(LOW)
    bias = key_bias(count, (branch.shape[0], 1), 0, 2 * rows)
    q = qkv[:, :features]
    k = qkv[:, features : 2 * features]
    v = qkv[:, 2 * features :]
    scale = head_dim**-0.5
    zero = jnp.zeros_like(q)
    totals = [jnp.zeros(q.shape, WIDE) for _ in range(3)]
    for h in range(heads):
        mine = head_mask(q.shape, h, head_dim)
        scores = dot_rt(k, jnp.where(mine, q, zero)) * scale + bias
        raw = jnp.exp(scores - jnp.max(scores, 0, keepdims=True))
        probs = raw * (1.0 / jnp.sum(raw, 0, keepdims=True))
        grad_probs = dot_rt(v, jnp.where(mine, g, zero))
        delta = jnp.sum(probs * grad_probs, 0, keepdims=True)
        grad_scores = (probs * (grad_probs - delta)).astype(LOW)
        totals[0] = jnp.where(mine, dot_lt(grad_scores, k) * scale, totals[0])
        totals[1] = jnp.where(mine, dot(grad_scores, q) * scale, totals[1])
        totals[2] = jnp.where(mine, dot(probs.astype(LOW), g), totals[2])
    for n in range(3):
        part = totals[n].astype(LOW)
        grad_qkv[:, n * features : (n + 1) * features] = part
        head_sums[0:1, n * features : (n + 1) * features] = jnp.sum(
            part.astype(WIDE), 0, keepdims=True
        )
    for i in range(ways):
        part = sum(
            dot_rt(
                grad_qkv[: 2 * rows, n * features : (n + 1) * features],
                third_of(packed[i], n, size, features),
            )
            for n in range(3)
        ).astype(LOW)
        keep[:, i * size : (i + 1) * size] = part[:rows]
        send[:, i * size : (i + 1) * size] = part[rows:]
    sums[...] = jnp.sum(branch[...].astype(WIDE), 0, keepdims=True)
    away[...] = dot_lt(normed[:, normed.shape[1] - away.shape[0] :], grad_qkv[...]).astype(LOW)


def first_sums_body(ways, grad_qkv, xhat, *refs):
    packed, out = refs[:ways], refs[ways]
    features = grad_qkv.shape[1] // 3
    size = xhat.shape[1] // ways
    for i in range(ways):
        part = sum(
            dot_rt(
                grad_qkv[:, n * features : (n + 1) * features],
                third_of(packed[i], n, size, features),
            )
            for n in range(3)
        )
        columns = slice(i * size, (i + 1) * size)
        out[0:1, columns] = jnp.sum(part * xhat[:, columns].astype(WIDE), 0, keepdims=True)
        out[1:2, columns] = jnp.sum(part, 0, keepdims=True)


def thirds_body(own, got, *outs):
    size = outs[0].shape[1]
    for n, out in enumerate(outs):
        columns = slice(n * size, (n + 1) * size)
        out[...] = own[:, columns] + got[:, columns].astype(WIDE)


def first_back_body(near, far, tokens, grad_hidden, vec, out):
    upstream = near[...].astype(WIDE) + far[...].astype(WIDE)
    grad, _ = norm_back_rows(tokens[...].astype(WIDE), vec[0:1, :], upstream)
    out[...] = grad + grad_hidden[...]


def on_device(
    tokens,
    cotangent,
    valid_count,
    gain_first,
    shift_first,
    query_weight,
    query_bias,
    key_weight,
    value_weight,
    value_bias,
    output_weight,
    output_bias,
    gain_second,
    shift_second,
    expand_weight,
    expand_bias,
    reduce_weight,
    reduce_bias,
):
    images, seq, width = tokens.shape
    ways = lax.axis_size("fsdp")
    pair = ways == 2
    parts = 2 if pair else 1
    cycle = lax.axis_size("context")
    mine = lax.axis_index("fsdp")
    place = lax.axis_index("context")
    core = lax.axis_index("tensor") & 1
    share = gain_first.shape[0]
    heads = query_bias.shape[1]
    head_dim = query_bias.shape[0] * ways
    features = heads * head_dim
    units = expand_weight.shape[1]
    half = seq // 2
    blocks = 2 * cycle
    length = cycle * seq
    second = mine == 1

    def turned(value):
        if not pair:
            return value
        left, right = jnp.split(value, 2, -1)
        return jnp.where(second, jnp.concatenate([right, left], -1), value)

    def piece_of(value, which):
        return turned(lax.dynamic_slice_in_dim(value.reshape(seq, width), which * half, half, 0))

    token_piece = piece_of(tokens, core)
    mine_tokens = spread_context(token_piece)
    token_pieces = woven(
        mine_tokens,
        [piece_of(tokens, 1 - core)] + [swap(m, "tensor", 1) for m in mine_tokens[1:]],
    )
    vectors = (gain_first, shift_first, output_bias, gain_second, shift_second, reduce_bias)
    biases = (query_bias, value_bias, expand_bias)
    thirds = (query_weight, key_weight, value_weight)

    if pair:
        across = lambda v: swap(v, "fsdp", 1)
        message, lines = kernel(
            pack_body,
            (low(share + 16, 3 * features), wide(16, 3 * features)),
            after(query_weight, token_piece),
            key_weight,
            value_weight,
            *vectors,
            *(b.T for b in biases),
            staged=True,
            limit=62,
        )
        first = across(message)
        packed = (message, first)
        output_parts = (output_weight, across(after(output_weight, message)))
        expand_parts = (expand_weight, across(after(expand_weight, first)))
        reduce_parts = (reduce_weight, across(after(reduce_weight, first)))
    else:
        gather = lambda v, axis=0: lax.all_gather(v, "fsdp", axis=axis, tiled=True)
        rows = [gather(v).reshape(1, -1) for v in vectors]
        rows += [gather(b).T.reshape(1, -1) for b in biases]
        lines = jnp.concatenate(
            [jnp.pad(r, ((0, 0), (0, width - r.shape[1]))) for r in rows]
            + [jnp.zeros((16 - len(rows), width), LOW)],
            0,
        ).astype(WIDE)
        packed = (jnp.concatenate([gather(w) for w in thirds], 1),)
        output_parts = (gather(output_weight, 1),)
        expand_parts = (gather(expand_weight),)
        reduce_parts = (gather(reduce_weight, 1),)

    vec, xhat_all, normed_all, qkv, context_own = kernel(
        lambda *refs: first_body(heads, head_dim, blocks, parts, *refs),
        (
            wide(16, width),
            low(length, width),
            low(length, width),
            low(length, 3 * features),
            low(seq, features),
        ),
        *token_pieces,
        *packed,
        lines,
        count=valid_count,
        flops=6 * length * width * features,
        moved=10 * length * width,
    )
    keep, send = kernel(
        lambda *refs: out_body(parts, *refs),
        (low(half, width), low(half, width)),
        context_own,
        *output_parts,
    )
    cot_piece = piece_of(cotangent, core)
    mine_cots = spread_context(after(cot_piece, mine_tokens[-1]))
    cots = woven(mine_cots, [swap(m, "tensor", 1) for m in mine_cots])
    near, far = last_terms(keep, send)
    near = after(near, *cots)
    hidden, normed_piece = kernel(
        second_body, (wide(half, width), low(half, width)), token_piece, near, far, vec
    )

    context_rest = kernel(
        lambda *refs: rest_body(heads, head_dim, seq, *refs),
        low(length - seq, features),
        after(qkv, near),
        count=valid_count,
    )
    mine_normed = spread_context(normed_piece)
    theirs = [swap(m, "tensor", 1) for m in mine_normed[:1]]
    mine_normed[1:] = [after(m, context_rest, expand_parts[-1]) for m in mine_normed[1:]]
    theirs += [swap(m, "tensor", 1) for m in mine_normed[1:]]
    (
        normed_two,
        cot_all,
        activated,
        grad_expanded,
        keep,
        send,
        out_keep,
        out_send,
        unit_sum,
        cot_sum,
    ) = kernel(
        lambda *refs: forward_body(blocks, parts, *refs),
        (low(length, width),) * 2
        + (low(length, units),) * 2
        + (low(half, width),) * 4
        + (wide(1, units), wide(1, width)),
        *woven(mine_normed, theirs),
        *cots,
        vec,
        *expand_parts,
        *reduce_parts,
        flops=10 * length * width * units,
        moved=12 * length * width,
        staged=True,
        limit=62,
    )
    near, far = last_terms(keep, send)
    grad_hidden, grad_piece, norm_sums = kernel(
        second_back_body,
        (wide(half, width), low(half, width), wide(2, width)),
        near,
        far,
        hidden,
        cot_piece,
        vec,
    )

    def scatter(value, axis):
        return lax.psum_scatter(value.astype(LOW), "fsdp", scatter_dimension=axis, tiled=True)

    def weight_grad(left, right, along):
        if not pair:
            return scatter(dot_lt(left, right), along).astype(WIDE)
        if along:
            own, other = segments(right, 2)
            away = across(dot_lt(left, other).astype(LOW))
            return pin(dot_lt(left, own)) + away.astype(WIDE)
        own, other = segments(left, 2)
        away = across(dot_lt(other, right).astype(LOW))
        return pin(dot_lt(own, right)) + away.astype(WIDE)

    if pair:
        many = units // 2
        act_half = lax.dynamic_slice_in_dim(activated, (place & 1) * many, many, 1)
        cot_own, cot_other = segments(cot_all, 2)
        normed_own, normed_other = segments(normed_two, 2)
        reduce_got = across(dot_lt(act_half, cot_other).astype(LOW))
        reduce_half = pin((dot_lt(act_half, cot_own) + reduce_got.astype(WIDE)).astype(LOW))
        expand_got = across(dot_lt(normed_other, grad_expanded).astype(LOW))
        grad_expand = pin(dot_lt(normed_own, grad_expanded)) + expand_got.astype(WIDE)

        def both_halves(value, theirs, axis):
            odd = (place & 1) != 0
            return jnp.concatenate(
                [jnp.where(odd, theirs, value), jnp.where(odd, value, theirs)], axis
            ).astype(WIDE)

    else:
        grad_reduce = weight_grad(activated, cot_all, 1)
        grad_expand = weight_grad(normed_two, grad_expanded, 0)

    mine_grads = spread_context(grad_piece)
    theirs = [swap(m, "tensor", 1) for m in mine_grads[:1]]
    if pair:
        mine_grads[1:] = [after(m, reduce_got) for m in mine_grads[1:]]
    theirs += [swap(m, "tensor", 1) for m in mine_grads[1:]]
    grad_branch, grad_qkv, keep, send, branch_sum, head_sum, away = kernel(
        lambda *refs: attend_back_body(heads, head_dim, blocks, parts, *refs),
        (
            low(length, width),
            low(length, 3 * features),
            low(half, width),
            low(half, width),
            wide(1, width),
            wide(1, 3 * features),
            low(width // parts, 3 * features),
        ),
        *woven(mine_grads, theirs),
        *output_parts,
        qkv,
        *packed,
        normed_all,
        count=valid_count,
        flops=10 * length * length * features,
        moved=8 * length * width,
    )
    if pair:
        qkv_got = across(away)
    near, far = last_terms(keep, send)
    if pair:
        reduce_theirs = swap(after(reduce_half, mine_grads[-1]), "context", 1)
        qkv_far = far
        near = after(near, reduce_theirs, expand_got, qkv_got)
        grad_reduce = both_halves(reduce_half, reduce_theirs, 0)
    grad_token_piece = kernel(
        first_back_body, wide(half, width), near, far, token_piece, grad_hidden, vec
    )

    def both_cores(value):
        theirs = swap(value, "tensor", 1)
        upper = core == 1
        return turned(
            jnp.concatenate([jnp.where(upper, theirs, value), jnp.where(upper, value, theirs)], 0)
        ).reshape(tokens.shape)

    grad_tokens = both_cores(grad_token_piece)

    if pair:
        grad_query, grad_key, grad_value = kernel(
            thirds_body,
            (wide(share, features),) * 3,
            dot_lt(segments(normed_all, 2)[0], grad_qkv),
            qkv_got,
        )
    else:
        grad_weights = scatter(dot_lt(normed_all, grad_qkv), 0).astype(WIDE)
        grad_query, grad_key, grad_value = jnp.split(grad_weights, 3, 1)

    near, far = last_terms(after(out_keep, grad_piece), after(out_send, grad_piece))
    reduced = near.astype(WIDE) + far.astype(WIDE) + vec[5:6, :]
    output = both_cores((hidden + reduced).astype(LOW))

    def own_rows(value):
        size = value.shape[0] // ways
        return lax.dynamic_slice_in_dim(value, mine * size, size, 0)

    context_all = jnp.concatenate([context_own, context_rest], 0)
    if pair:
        context_all = after(context_all, qkv_far)
    grad_output = weight_grad(context_all, grad_branch, 1)

    first_sums = kernel(
        lambda *refs: first_sums_body(parts, *refs), wide(2, width), grad_qkv, xhat_all, *packed
    )
    bit = 1
    while bit < lax.axis_size("tensor"):
        first_sums = first_sums + swap(first_sums, "tensor", bit)
        bit *= 2
    norm_sums = after(norm_sums, mine_grads[-1])
    norm_sums = norm_sums + swap(norm_sums, "tensor", 1)
    bit = 1
    while bit < cycle:
        norm_sums = norm_sums + swap(norm_sums, "context", bit)
        bit *= 2
    sums = jnp.concatenate([first_sums, norm_sums, branch_sum, cot_sum], 0)
    plain = jnp.concatenate(
        [jnp.pad(head_sum, ((0, 0), (0, width - 3 * features))), unit_sum], 0
    )
    if pair:
        own, other = segments(sums, 2)
        got = across(jnp.concatenate([other, *segments(plain, 2)], 0))
        sums = own + got[:6]
        plain = plain + jnp.concatenate([got[6:8], got[8:10]], 1)
    else:
        sums = scatter(sums, 1).astype(WIDE)
        plain = lax.psum(plain, "fsdp")
    grad_ebias = own_rows(plain[1].reshape(-1, expand_bias.shape[0] * ways).T)
    grad_qbias, grad_vbias = (
        own_rows(plain[0, n * features : (n + 1) * features].reshape(heads, head_dim).T)
        for n in (0, 2)
    )
    return (
        output,
        grad_tokens,
        sums[0],
        sums[1],
        grad_query,
        grad_qbias,
        grad_key,
        grad_value,
        grad_vbias,
        grad_output,
        sums[4],
        sums[2],
        sums[3],
        grad_expand,
        grad_ebias,
        grad_reduce,
        sums[5],
    )


def solution(mesh):
    rows = P("fsdp", "context", None)
    vector = P("fsdp")
    split = P("fsdp", "tensor")
    turned = P("tensor", "fsdp")
    in_specs = (rows, rows, vector, vector, vector, split, split, split, split, split)
    in_specs += (turned, vector, vector, vector, split, split, turned, vector)
    out_specs = (rows, rows, vector, vector, split, split, split, split, split)
    out_specs += (turned, vector, vector, vector, split, split, turned, vector)
    return jax.shard_map(
        on_device, mesh=mesh, in_specs=in_specs, out_specs=out_specs, check_vma=False
    )
```

```python
import jax
import jax.numpy as jnp
from jax import lax
from jax.experimental import pallas as pl
from jax.experimental.pallas import tpu as pltpu
from jax.sharding import PartitionSpec as P

EPS = 1e-06
LOW = jnp.bfloat16
WIDE = jnp.float32


def swap(block, axis, bit):
    return lax.ppermute(block, axis, [(i, i ^ bit) for i in range(lax.axis_size(axis))])


def after(value, *others):
    return lax.optimization_barrier((value, *others))[0]


def pin(value):
    return lax.optimization_barrier(value)


def dot(left, right):
    return lax.dot_general(left, right, (((1,), (0,)), ((), ())), preferred_element_type=WIDE)


def dot_rt(left, right):
    return lax.dot_general(left, right, (((1,), (1,)), ((), ())), preferred_element_type=WIDE)


def dot_lt(left, right):
    return lax.dot_general(left, right, (((0,), (0,)), ((), ())), preferred_element_type=WIDE)


def segments(value, count):
    size = value.shape[1] // count
    return [value[:, i * size : (i + 1) * size] for i in range(count)]


def sum_cores(keep, send):
    return (keep.astype(WIDE) + swap(send, "tensor", 1).astype(WIDE)).astype(LOW)


def last_terms(keep, send):
    value = pin(sum_cores(keep, send))
    bit = 2
    while True:
        got = swap(value, "tensor", bit)
        bit *= 2
        if bit >= lax.axis_size("tensor"):
            return value, got
        value = pin((value.astype(WIDE) + got.astype(WIDE)).astype(LOW))


def spread_context(piece):
    return [piece] + [swap(piece, "context", k) for k in range(1, lax.axis_size("context"))]


def woven(mine, theirs):
    return [block for both in zip(mine, theirs) for block in both]


class Late:
    def __init__(self, ref, copy):
        self.ref, self.copy, self.shape = ref, copy, ref.shape

    def wait(self):
        if self.copy is not None:
            self.copy.wait()
            self.copy = None

    def __getitem__(self, index):
        self.wait()
        return self.ref[index]


def kernel(body, out_shape, *args, count=None, flops=0, moved=0, staged=False, limit=48):
    scalars = [] if count is None else [count]
    first, last = len(scalars), len(scalars) + len(args)

    def run(*refs):
        buffers, arrived = refs[-len(args) - 1 : -1], refs[-1]
        inputs = []
        for n, (source, buffer) in enumerate(zip(refs[first:last], buffers)):
            copy = pltpu.make_async_copy(source, buffer, arrived.at[n])
            copy.start()
            inputs.append(Late(buffer, copy))
        body(*refs[:first], *inputs, *refs[last : -len(args) - 1])
        for late in inputs:
            late.wait()

    scratch = [pltpu.VMEM(a.shape, a.dtype) for a in args] + [pltpu.SemaphoreType.DMA((len(args),))]
    space = pltpu.HBM if staged else pltpu.VMEM
    return pl.pallas_call(
        run if staged else body,
        out_shape=out_shape,
        in_specs=[pl.BlockSpec(memory_space=pltpu.SMEM)] * first
        + [pl.BlockSpec(memory_space=space)] * len(args),
        scratch_shapes=scratch if staged else (),
        compiler_params=pltpu.CompilerParams(vmem_limit_bytes=limit << 20),
        cost_estimate=pl.CostEstimate(flops=flops, bytes_accessed=moved, transcendentals=0),
    )(*scalars, *args)


def low(*shape):
    return jax.ShapeDtypeStruct(shape, LOW)


def wide(*shape):
    return jax.ShapeDtypeStruct(shape, WIDE)


QBIAS, VBIAS, EBIAS = 6, 7, 8
FIRST_COST = 20_000_000_000


def pack_body(*refs):
    weights, vectors, biases = refs[:3], refs[3:9], refs[9:12]
    message, lines = refs[12:]
    ways = lax.axis_size("fsdp")
    mine = lax.axis_index("fsdp")
    share, columns = weights[0].shape
    lines[...] = jnp.zeros_like(lines)
    for n, ref in enumerate(vectors):
        lines[n : n + 1, :share] = ref[...].reshape(1, -1).astype(WIDE)
    for n, ref in zip((QBIAS, VBIAS, EBIAS), biases):
        groups, size = ref.shape
        each = size * ways
        row = lax.broadcasted_iota(jnp.int32, (size, groups * each), 0)
        column = lax.broadcasted_iota(jnp.int32, (size, groups * each), 1)
        within = column
        for g in range(1, groups):
            within = jnp.where(column >= g * each, column - g * each, within)
        tiled = dot(ref[...], (within == row + mine * size).astype(LOW))
        group = lax.broadcasted_iota(jnp.int32, tiled.shape, 0)
        column = lax.broadcasted_iota(jnp.int32, tiled.shape, 1)
        keep = (column >= group * each) & (column < (group + 1) * each)
        flat = jnp.sum(jnp.where(keep, tiled, 0.0), 0, keepdims=True)
        for at in range(0, groups * each, share):
            part = flat[:, at : at + share]
            lines[n + at // share : n + at // share + 1, : part.shape[1]] = part
    message[share:, :] = lines[...].astype(LOW)
    for n, w in enumerate(weights):
        message[:share, n * columns : (n + 1) * columns] = w[...]


def merge(own, got, out):
    share = out.shape[1] // 2
    out[...] = jnp.zeros_like(out)
    mine, theirs = own[...], got[got.shape[0] - own.shape[0] :, :].astype(WIDE)
    out[:QBIAS, :share] = mine[:QBIAS, :share]
    out[:QBIAS, share:] = theirs[:QBIAS, :share]
    both = mine + theirs
    out[QBIAS : EBIAS + 1, :share] = both[QBIAS : EBIAS + 1, :share]
    out[EBIAS : EBIAS + 1, share:] = both[EBIAS + 1 : EBIAS + 2, :share]


def normed_rows(values):
    center = values - jnp.mean(values, -1, keepdims=True)
    return center * lax.rsqrt(jnp.mean(center * center, -1, keepdims=True) + EPS)


def norm_back_rows(values, gain, upstream):
    center = values - jnp.mean(values, -1, keepdims=True)
    spread = lax.rsqrt(jnp.mean(center * center, -1, keepdims=True) + EPS)
    xhat = center * spread
    z = upstream * gain
    grad = spread * (
        z - jnp.mean(z, -1, keepdims=True) - xhat * jnp.mean(z * xhat, -1, keepdims=True)
    )
    return grad, xhat


def third_of(message, n, size, features):
    return message[:size, n * features : (n + 1) * features]


def key_bias(count, shape, axis, seq):
    step = lax.broadcasted_iota(jnp.int32, shape, axis)
    place = lax.axis_index("context")
    core = lax.axis_index("tensor") & 1
    half = seq // 2
    position = step
    for b in range(shape[axis] // half):
        start = (place ^ (b // 2)) * seq + (core ^ (b % 2)) * half
        position = jnp.where(step >= b * half, step + (start - b * half), position)
    return jnp.where(position < count[0], 0.0, -1e30).astype(WIDE)


def head_mask(shape, head, head_dim):
    lane = lax.broadcasted_iota(jnp.int32, shape, 1)
    return (lane >= head * head_dim) & (lane < (head + 1) * head_dim)


def attend_rows(heads, head_dim, start, rows, qkv, bias):
    features = heads * head_dim
    q = qkv[start : start + rows, :features]
    k = qkv[:, features : 2 * features]
    v = qkv[:, 2 * features :]
    scale = head_dim**-0.5
    total = jnp.zeros((rows, features), WIDE)
    for h in range(heads):
        mine = head_mask(q.shape, h, head_dim)
        scores = dot_rt(jnp.where(mine, q, jnp.zeros_like(q)), k) * scale + bias
        raw = jnp.exp(scores - jnp.max(scores, -1, keepdims=True))
        got = dot(raw.astype(LOW), v) / jnp.sum(raw, -1, keepdims=True)
        total = jnp.where(mine, got, total)
    return total.astype(LOW)


def first_body(heads, head_dim, blocks, ways, count, *refs):
    pieces, refs = refs[:blocks], refs[blocks:]
    packed, lines, refs = refs[:ways], refs[ways], refs[ways + 1 :]
    vec, xhat, normed, qkv, context = refs
    rows = pieces[0].shape[0]
    if ways == 2:
        merge(lines, packed[1], vec)
    else:
        vec[...] = lines[...]
    features = heads * head_dim
    for n, piece in enumerate(pieces):
        part = normed_rows(piece[...].astype(WIDE))
        xhat[n * rows : (n + 1) * rows, :] = part.astype(LOW)
        normed[n * rows : (n + 1) * rows, :] = (part * vec[0:1, :] + vec[1:2, :]).astype(LOW)
    size = normed.shape[1] // ways
    for n, row in enumerate((QBIAS, None, VBIAS)):
        got = sum(
            dot(normed[:, i * size : (i + 1) * size], third_of(w, n, size, features))
            for i, w in enumerate(packed)
        )
        if row is not None:
            got = got + vec[row : row + 1, :features]
        qkv[:, n * features : (n + 1) * features] = got.astype(LOW)
    bias = key_bias(count, (1, blocks * rows), 1, 2 * rows)
    context[...] = attend_rows(heads, head_dim, 0, 2 * rows, qkv, bias)


def out_body(ways, *refs):
    context, weights, (keep, send) = refs[0], refs[1 : 1 + ways], refs[1 + ways :]
    rows, size = keep.shape[0], keep.shape[1] // ways
    for i, w in enumerate(weights):
        part = dot(context[...], w[...]).astype(LOW)
        keep[:, i * size : (i + 1) * size] = part[:rows]
        send[:, i * size : (i + 1) * size] = part[rows:]


def rest_body(heads, head_dim, start, count, qkv, out):
    bias = key_bias(count, (1, qkv.shape[0]), 1, start)
    out[...] = attend_rows(heads, head_dim, start, out.shape[0], qkv, bias)


def second_body(tokens, near, far, vec, hidden, normed):
    total = tokens[...].astype(WIDE) + (near[...].astype(WIDE) + far[...].astype(WIDE))
    total = total + vec[2:3, :]
    hidden[...] = total
    normed[...] = (normed_rows(total) * vec[3:4, :] + vec[4:5, :]).astype(LOW)


def forward_body(blocks, ways, *refs):
    normed, cots, refs = refs[:blocks], refs[blocks : 2 * blocks], refs[2 * blocks :]
    vec, expand, reduce = refs[0], refs[1 : 1 + ways], refs[1 + ways : 1 + 2 * ways]
    normed_all, cot_all, act, grad, keep, send, out_keep, out_send, unit_sum, cot_sum, *aways = refs[
        1 + 2 * ways :
    ]
    rows = normed[0].shape[0]
    size = normed_all.shape[1] // ways
    units = act.shape[1]
    place = lax.axis_index("context")
    for n in range(blocks):
        normed_all[n * rows : (n + 1) * rows, :] = normed[n][...]
    for n in range(blocks):
        cot_all[n * rows : (n + 1) * rows, :] = cots[n][...]
    cot_sum[...] = jnp.sum(cot_all[...].astype(WIDE), 0, keepdims=True)
    step = min(256, units, size)
    back = [jnp.zeros((2 * rows, size), WIDE) for _ in range(ways)]
    out = [jnp.zeros((2 * rows, size), WIDE) for _ in range(ways)]
    for at in range(0, units, step):
        columns = slice(at, at + step)
        expands = [w[:, columns] for w in expand]
        reduces = [w[columns, :] for w in reduce]
        sides = [slice(i * size, (i + 1) * size) for i in range(ways)]
        value = sum(dot(normed_all[:, c], w) for c, w in zip(sides, expands))
        value = value + vec[EBIAS : EBIAS + 1, columns]
        cdf = 0.5 * (1.0 + lax.erf(value * (2.0**-0.5)))
        act[:, columns] = (value * cdf).astype(LOW)
        slope = cdf + value * jnp.exp(-0.5 * value * value) * 0.3989422804014327
        part = sum(dot_rt(cot_all[:, c], w) for c, w in zip(sides, reduces))
        part = (part * slope).astype(LOW)
        grad[:, columns] = part
        unit_sum[0:1, columns] = jnp.sum(part.astype(WIDE), 0, keepdims=True)
        own = act[: 2 * rows, columns]
        for i in range(ways):
            back[i] = back[i] + dot_rt(part[: 2 * rows], expands[i])
            out[i] = out[i] + dot(own, reduces[i])
    for i, c in enumerate(sides):
        keep[:, c] = back[i][:rows].astype(LOW)
        send[:, c] = back[i][rows:].astype(LOW)
        out_keep[:, c] = out[i][:rows].astype(LOW)
        out_send[:, c] = out[i][rows:].astype(LOW)
    if aways:
        many = units // 2
        chosen = pl.ds(pl.multiple_of((place & 1) * many, many), many)
        aways[0][...] = dot_lt(act[:, chosen], cot_all[:, size:]).astype(LOW)
        aways[1][...] = dot_lt(normed_all[:, size:], grad[...]).astype(LOW)


def second_back_body(near, far, hidden, cot, vec, grad_hidden, grad_branch):
    upstream = near[...].astype(WIDE) + far[...].astype(WIDE)
    grad, xhat = norm_back_rows(hidden[...], vec[3:4, :], upstream)
    total = grad + cot[...].astype(WIDE)
    grad_hidden[...] = total
    rows = total.shape[0]
    grad_branch[:rows, :] = total.astype(LOW)
    below = jnp.zeros((grad_branch.shape[0] - rows, total.shape[1]), WIDE)
    line = lax.broadcasted_iota(jnp.int32, below.shape, 0)
    below = jnp.where(line == 0, jnp.sum(upstream * xhat, 0, keepdims=True), below)
    below = jnp.where(line == 1, jnp.sum(upstream, 0, keepdims=True), below)
    grad_branch[rows:, :] = below.astype(LOW)


def attend_back_body(heads, head_dim, blocks, ways, count, *refs):
    pieces, refs = refs[:blocks], refs[blocks:]
    outs, qkv, packed = refs[:ways], refs[ways], refs[ways + 1 : 2 * ways + 1]
    normed, contexts = refs[2 * ways + 1], refs[2 * ways + 2 : 2 * ways + 4]
    branch, grad_qkv, keep, send, sums, norm_sums, head_sums, away = refs[2 * ways + 4 :]
    rows = keep.shape[0]
    features = heads * head_dim
    below = jnp.zeros((pieces[0].shape[0] - rows, branch.shape[1]), WIDE)
    for n, piece in enumerate(pieces):
        branch[n * rows : (n + 1) * rows, :] = piece[:rows, :]
        below = below + piece[rows:, :].astype(WIDE)
    norm_sums[...] = below[:2]
    size = branch.shape[1] // ways
    g = sum(
        dot_rt(branch[:, i * size : (i + 1) * size], w[...]) for i, w in enumerate(outs)
    ).astype(LOW)
    bias = key_bias(count, (branch.shape[0], 1), 0, 2 * rows)
    q = qkv[:, :features]
    k = qkv[:, features : 2 * features]
    v = qkv[:, 2 * features :]
    scale = head_dim**-0.5
    zero = jnp.zeros_like(q)
    totals = [jnp.zeros(q.shape, WIDE) for _ in range(3)]
    for h in range(heads):
        mine = head_mask(q.shape, h, head_dim)
        scores = dot_rt(k, jnp.where(mine, q, zero)) * scale + bias
        raw = jnp.exp(scores - jnp.max(scores, 0, keepdims=True))
        probs = raw * (1.0 / jnp.sum(raw, 0, keepdims=True))
        grad_probs = dot_rt(v, jnp.where(mine, g, zero))
        delta = jnp.sum(probs * grad_probs, 0, keepdims=True)
        grad_scores = (probs * (grad_probs - delta)).astype(LOW)
        totals[0] = jnp.where(mine, dot_lt(grad_scores, k) * scale, totals[0])
        totals[1] = jnp.where(mine, dot(grad_scores, q) * scale, totals[1])
        totals[2] = jnp.where(mine, dot(probs.astype(LOW), g), totals[2])
    for n in range(3):
        part = totals[n].astype(LOW)
        grad_qkv[:, n * features : (n + 1) * features] = part
        head_sums[0:1, n * features : (n + 1) * features] = jnp.sum(
            part.astype(WIDE), 0, keepdims=True
        )
    for i in range(ways):
        part = sum(
            dot_rt(
                grad_qkv[: 2 * rows, n * features : (n + 1) * features],
                third_of(packed[i], n, size, features),
            )
            for n in range(3)
        ).astype(LOW)
        keep[:, i * size : (i + 1) * size] = part[:rows]
        send[:, i * size : (i + 1) * size] = part[rows:]
    sums[...] = jnp.sum(branch[...].astype(WIDE), 0, keepdims=True)
    other = normed.shape[1] - away.shape[0]
    away[:, : 3 * features] = dot_lt(normed[:, other:], grad_qkv[...]).astype(LOW)
    first = contexts[0].shape[0]
    part = dot_lt(contexts[0][...], branch[:first, other:])
    part = (part + dot_lt(contexts[1][...], branch[first:, other:])).astype(LOW)
    for n in range(away.shape[0] // features):
        away[n * features : (n + 1) * features, 3 * features :] = part[
            :, n * features : (n + 1) * features
        ]


def first_sums_body(ways, grad_qkv, xhat, *refs):
    packed, out = refs[:ways], refs[ways]
    features = grad_qkv.shape[1] // 3
    size = xhat.shape[1] // ways
    for i in range(ways):
        part = sum(
            dot_rt(
                grad_qkv[:, n * features : (n + 1) * features],
                third_of(packed[i], n, size, features),
            )
            for n in range(3)
        )
        columns = slice(i * size, (i + 1) * size)
        out[0:1, columns] = jnp.sum(part * xhat[:, columns].astype(WIDE), 0, keepdims=True)
        out[1:2, columns] = jnp.sum(part, 0, keepdims=True)


def last_body(own, own_out, got, query, key, value, out):
    size = query.shape[1]
    for n, ref in enumerate((query, key, value)):
        columns = slice(n * size, (n + 1) * size)
        ref[...] = own[:, columns] + got[:, columns].astype(WIDE)
    for n in range(out.shape[1] // size):
        columns = slice(n * size, (n + 1) * size)
        out[:, columns] = own_out[:, columns] + got[columns, 3 * size :].astype(WIDE)


def first_back_body(near, far, tokens, grad_hidden, vec, out):
    upstream = near[...].astype(WIDE) + far[...].astype(WIDE)
    grad, _ = norm_back_rows(tokens[...].astype(WIDE), vec[0:1, :], upstream)
    out[...] = grad + grad_hidden[...]


def on_device(
    tokens,
    cotangent,
    valid_count,
    gain_first,
    shift_first,
    query_weight,
    query_bias,
    key_weight,
    value_weight,
    value_bias,
    output_weight,
    output_bias,
    gain_second,
    shift_second,
    expand_weight,
    expand_bias,
    reduce_weight,
    reduce_bias,
):
    images, seq, width = tokens.shape
    ways = lax.axis_size("fsdp")
    pair = ways == 2
    parts = 2 if pair else 1
    cycle = lax.axis_size("context")
    mine = lax.axis_index("fsdp")
    place = lax.axis_index("context")
    core = lax.axis_index("tensor") & 1
    share = gain_first.shape[0]
    heads = query_bias.shape[1]
    head_dim = query_bias.shape[0] * ways
    features = heads * head_dim
    units = expand_weight.shape[1]
    half = seq // 2
    blocks = 2 * cycle
    length = cycle * seq
    second = mine == 1

    def turned(value):
        if not pair:
            return value
        left, right = jnp.split(value, 2, -1)
        return jnp.where(second, jnp.concatenate([right, left], -1), value)

    def piece_of(value, which):
        return turned(lax.dynamic_slice_in_dim(value.reshape(seq, width), which * half, half, 0))

    token_piece = piece_of(tokens, core)
    vectors = (gain_first, shift_first, output_bias, gain_second, shift_second, reduce_bias)
    biases = (query_bias, value_bias, expand_bias)
    thirds = (query_weight, key_weight, value_weight)

    if pair:
        across = lambda v: swap(v, "fsdp", 1)
        message, lines = kernel(
            pack_body,
            (low(share + 16, 3 * features), wide(16, 3 * features)),
            after(query_weight, token_piece),
            key_weight,
            value_weight,
            *vectors,
            *(b.T for b in biases),
            staged=True,
            limit=62,
        )
        first = across(message)
        packed = (message, first)
        output_parts = (output_weight, across(after(output_weight, message)))
        reduce_parts = (reduce_weight, across(after(reduce_weight, first)))
    else:
        gather = lambda v, axis=0: lax.all_gather(v, "fsdp", axis=axis, tiled=True)
        rows = [gather(v).reshape(1, -1) for v in vectors]
        rows += [gather(b).T.reshape(1, -1) for b in biases]
        lines = jnp.concatenate(
            [jnp.pad(r, ((0, 0), (0, width - r.shape[1]))) for r in rows]
            + [jnp.zeros((16 - len(rows), width), LOW)],
            0,
        ).astype(WIDE)
        packed = (jnp.concatenate([gather(w) for w in thirds], 1),)
        output_parts = (gather(output_weight, 1),)
        expand_parts = (gather(expand_weight),)
        reduce_parts = (gather(reduce_weight, 1),)

    mine_tokens = spread_context(token_piece)
    token_pieces = woven(
        mine_tokens,
        [piece_of(tokens, 1 - core)]
        + [swap(after(m, packed[-1]), "tensor", 1) for m in mine_tokens[1:]],
    )
    cot_piece = piece_of(cotangent, core)
    mine_cots = spread_context(after(cot_piece, *mine_tokens[1:]))
    mine_cots = list(lax.optimization_barrier(tuple(mine_cots)))
    if pair:
        expand_parts = (expand_weight, across(after(expand_weight, mine_tokens[1])))

    vec, xhat_all, normed_all, qkv, context_own = kernel(
        lambda *refs: first_body(heads, head_dim, blocks, parts, *refs),
        (
            wide(16, width),
            low(length, width),
            low(length, width),
            low(length, 3 * features),
            low(seq, features),
        ),
        *token_pieces,
        *packed,
        lines,
        count=valid_count,
        flops=FIRST_COST,
    )
    keep, send = kernel(
        lambda *refs: out_body(parts, *refs),
        (low(half, width), low(half, width)),
        context_own,
        *output_parts,
    )
    near, far = last_terms(keep, send)
    far, *mine_cots = lax.optimization_barrier((far, *mine_cots))
    far = after(far, expand_parts[-1])
    cots = woven(mine_cots, [swap(m, "tensor", 1) for m in mine_cots])
    hidden, normed_piece = kernel(
        second_body, (wide(half, width), low(half, width)), token_piece, near, far, vec
    )

    context_rest = kernel(
        lambda *refs: rest_body(heads, head_dim, seq, *refs),
        low(length - seq, features),
        after(qkv, near),
        count=valid_count,
    )
    mine_normed = spread_context(normed_piece)
    theirs = [swap(m, "tensor", 1) for m in mine_normed[:1]]
    mine_normed[1:] = [after(m, context_rest, expand_parts[-1]) for m in mine_normed[1:]]
    theirs += [swap(m, "tensor", 1) for m in mine_normed[1:]]
    (
        normed_two,
        cot_all,
        activated,
        grad_expanded,
        keep,
        send,
        out_keep,
        out_send,
        unit_sum,
        cot_sum,
        *aways,
    ) = kernel(
        lambda *refs: forward_body(blocks, parts, *refs),
        (low(length, width),) * 2
        + (low(length, units),) * 2
        + (low(half, width),) * 4
        + (wide(1, units), wide(1, width))
        + ((low(units // 2, share), low(share, units)) if pair else ()),
        *woven(mine_normed, theirs),
        *cots,
        vec,
        *expand_parts,
        *reduce_parts,
        flops=10 * length * width * units,
        moved=12 * length * width,
        staged=True,
        limit=62,
    )
    near, far = last_terms(keep, send)
    if pair:
        many = units // 2
        act_half = lax.dynamic_slice_in_dim(activated, (place & 1) * many, many, 1)
        cot_own, normed_own = segments(cot_all, 2)[0], segments(normed_two, 2)[0]
    grad_hidden, grad_piece = kernel(
        second_back_body,
        (wide(half, width), low(half + 16, width)),
        near,
        far,
        hidden,
        cot_piece,
        vec,
    )

    def scatter(value, axis):
        return lax.psum_scatter(value.astype(LOW), "fsdp", scatter_dimension=axis, tiled=True)

    def weight_grad(left, right, along):
        if not pair:
            return scatter(dot_lt(left, right), along).astype(WIDE)
        if along:
            own, other = segments(right, 2)
            away = across(dot_lt(left, other).astype(LOW))
            return pin(dot_lt(left, own)) + away.astype(WIDE)
        own, other = segments(left, 2)
        away = across(dot_lt(other, right).astype(LOW))
        return pin(dot_lt(own, right)) + away.astype(WIDE)

    if pair:
        reduce_got, expand_got = (across(a) for a in aways)

        def both_halves(value, theirs, axis):
            odd = (place & 1) != 0
            return jnp.concatenate(
                [jnp.where(odd, theirs, value), jnp.where(odd, value, theirs)], axis
            ).astype(WIDE)

    else:
        grad_reduce = weight_grad(activated, cot_all, 1)
        grad_expand = weight_grad(normed_two, grad_expanded, 0)

    mine_grads = spread_context(grad_piece)
    out_near, out_far = last_terms(after(out_keep, grad_piece), after(out_send, grad_piece))
    ready = [out_far]
    theirs = [swap(m, "tensor", 1) for m in mine_grads[:1]]
    if pair:
        *mine_grads[1:], reduce_got = lax.optimization_barrier((*mine_grads[1:], reduce_got))
        reduce_half = pin((dot_lt(act_half, cot_own) + reduce_got.astype(WIDE)).astype(LOW))
        expand_own = pin(dot_lt(after(normed_own, grad_piece), grad_expanded))
        ready += [reduce_half, expand_own]
    theirs += [swap(m, "tensor", 1) for m in mine_grads[1:]]
    grad_branch, grad_qkv, keep, send, branch_sum, norm_sums, head_sum, away = kernel(
        lambda *refs: attend_back_body(heads, head_dim, blocks, parts, *refs),
        (
            low(length, width),
            low(length, 3 * features),
            low(half, width),
            low(half, width),
            wide(1, width),
            wide(2, width),
            wide(1, 3 * features),
            low(width // parts, 4 * features),
        ),
        *woven(mine_grads, theirs),
        *output_parts,
        after(qkv, *ready),
        *packed,
        normed_all,
        context_own,
        context_rest,
        count=valid_count,
        flops=10 * length * length * features,
        moved=8 * length * width,
    )
    if pair:
        qkv_got = across(away)
    if pair:
        send = after(send, expand_got)
    near, far = last_terms(keep, send)
    gn_far = far
    if pair:
        grad_reduce = both_halves(
            reduce_half, swap(after(reduce_half, head_sum), "context", 1), 0
        )
        grad_expand = expand_own + expand_got.astype(WIDE)
    grad_token_piece = kernel(
        first_back_body, wide(half, width), near, far, token_piece, grad_hidden, vec
    )

    def both_cores(value):
        theirs = swap(value, "tensor", 1)
        upper = core == 1
        return turned(
            jnp.concatenate([jnp.where(upper, theirs, value), jnp.where(upper, value, theirs)], 0)
        ).reshape(tokens.shape)

    grad_tokens = both_cores(grad_token_piece)

    reduced = out_near.astype(WIDE) + out_far.astype(WIDE) + vec[5:6, :]
    output = both_cores((hidden + reduced).astype(LOW))

    if pair:
        grad_query, grad_key, grad_value, grad_output = kernel(
            last_body,
            (wide(share, features),) * 3 + (wide(features, share),),
            dot_lt(segments(normed_all, 2)[0], after(grad_qkv, gn_far)),
            dot_lt(jnp.concatenate([context_own, context_rest], 0), after(segments(grad_branch, 2)[0], gn_far)),
            qkv_got,
        )
    else:
        grad_weights = scatter(dot_lt(normed_all, grad_qkv), 0).astype(WIDE)
        grad_query, grad_key, grad_value = jnp.split(grad_weights, 3, 1)
        context_all = jnp.concatenate([context_own, context_rest], 0)
        grad_output = scatter(dot_lt(context_all, grad_branch), 1).astype(WIDE)

    def own_rows(value):
        size = value.shape[0] // ways
        return lax.dynamic_slice_in_dim(value, mine * size, size, 0)

    first_sums = kernel(
        lambda *refs: first_sums_body(parts, *refs), wide(2, width), after(grad_qkv, gn_far), xhat_all, *packed
    )
    bit = 1
    while bit < lax.axis_size("tensor"):
        first_sums = first_sums + swap(first_sums, "tensor", bit)
        bit *= 2
    sums = jnp.concatenate([first_sums, norm_sums, branch_sum, cot_sum], 0)
    plain = jnp.concatenate(
        [jnp.pad(head_sum, ((0, 0), (0, width - 3 * features))), unit_sum], 0
    )
    if pair:
        own, other = segments(sums, 2)
        got = across(jnp.concatenate([other, *segments(plain, 2)], 0))
        sums = own + got[:6]
        plain = plain + jnp.concatenate([got[6:8], got[8:10]], 1)
    else:
        sums = scatter(sums, 1).astype(WIDE)
        plain = lax.psum(plain, "fsdp")
    grad_ebias = own_rows(plain[1].reshape(-1, expand_bias.shape[0] * ways).T)
    grad_qbias, grad_vbias = (
        own_rows(plain[0, n * features : (n + 1) * features].reshape(heads, head_dim).T)
        for n in (0, 2)
    )
    return (
        output,
        grad_tokens,
        sums[0],
        sums[1],
        grad_query,
        grad_qbias,
        grad_key,
        grad_value,
        grad_vbias,
        grad_output,
        sums[4],
        sums[2],
        sums[3],
        grad_expand,
        grad_ebias,
        grad_reduce,
        sums[5],
    )


def solution(mesh):
    rows = P("fsdp", "context", None)
    vector = P("fsdp")
    split = P("fsdp", "tensor")
    turned = P("tensor", "fsdp")
    in_specs = (rows, rows, vector, vector, vector, split, split, split, split, split)
    in_specs += (turned, vector, vector, vector, split, split, turned, vector)
    out_specs = (rows, rows, vector, vector, split, split, split, split, split)
    out_specs += (turned, vector, vector, vector, split, split, turned, vector)
    return jax.shard_map(
        on_device, mesh=mesh, in_specs=in_specs, out_specs=out_specs, check_vma=False
    )
```

```python
import jax
import jax.numpy as jnp
from jax import lax
from jax.experimental import pallas as pl
from jax.experimental.pallas import tpu as pltpu
from jax.sharding import PartitionSpec as P

EPS = 1e-06
LOW = jnp.bfloat16
WIDE = jnp.float32


def swap(block, axis, bit):
    return lax.ppermute(block, axis, [(i, i ^ bit) for i in range(lax.axis_size(axis))])


def after(value, *others):
    return lax.optimization_barrier((value, *others))[0]


def pin(value):
    return lax.optimization_barrier(value)


def dot(left, right):
    return lax.dot_general(left, right, (((1,), (0,)), ((), ())), preferred_element_type=WIDE)


def dot_rt(left, right):
    return lax.dot_general(left, right, (((1,), (1,)), ((), ())), preferred_element_type=WIDE)


def dot_lt(left, right):
    return lax.dot_general(left, right, (((0,), (0,)), ((), ())), preferred_element_type=WIDE)


def segments(value, count):
    size = value.shape[1] // count
    return [value[:, i * size : (i + 1) * size] for i in range(count)]


def sum_cores(keep, send):
    return (keep.astype(WIDE) + swap(send, "tensor", 1).astype(WIDE)).astype(LOW)


def last_terms(keep, send):
    value = pin(sum_cores(keep, send))
    bit = 2
    while True:
        got = swap(value, "tensor", bit)
        bit *= 2
        if bit >= lax.axis_size("tensor"):
            return value, got
        value = pin((value.astype(WIDE) + got.astype(WIDE)).astype(LOW))


def spread_context(piece):
    return [piece] + [swap(piece, "context", k) for k in range(1, lax.axis_size("context"))]


def woven(mine, theirs):
    return [block for both in zip(mine, theirs) for block in both]


class Late:
    def __init__(self, ref, copy):
        self.ref, self.copy, self.shape = ref, copy, ref.shape

    def wait(self):
        if self.copy is not None:
            self.copy.wait()
            self.copy = None

    def __getitem__(self, index):
        self.wait()
        return self.ref[index]


def kernel(body, out_shape, *args, count=None, flops=0, moved=0, staged=False, limit=48):
    scalars = [] if count is None else [count]
    first, last = len(scalars), len(scalars) + len(args)

    def run(*refs):
        buffers, arrived = refs[-len(args) - 1 : -1], refs[-1]
        inputs = []
        for n, (source, buffer) in enumerate(zip(refs[first:last], buffers)):
            copy = pltpu.make_async_copy(source, buffer, arrived.at[n])
            copy.start()
            inputs.append(Late(buffer, copy))
        body(*refs[:first], *inputs, *refs[last : -len(args) - 1])
        for late in inputs:
            late.wait()

    scratch = [pltpu.VMEM(a.shape, a.dtype) for a in args] + [pltpu.SemaphoreType.DMA((len(args),))]
    space = pltpu.HBM if staged else pltpu.VMEM
    return pl.pallas_call(
        run if staged else body,
        out_shape=out_shape,
        in_specs=[pl.BlockSpec(memory_space=pltpu.SMEM)] * first
        + [pl.BlockSpec(memory_space=space)] * len(args),
        scratch_shapes=scratch if staged else (),
        compiler_params=pltpu.CompilerParams(vmem_limit_bytes=limit << 20),
        cost_estimate=pl.CostEstimate(flops=flops, bytes_accessed=moved, transcendentals=0),
    )(*scalars, *args)


def low(*shape):
    return jax.ShapeDtypeStruct(shape, LOW)


def wide(*shape):
    return jax.ShapeDtypeStruct(shape, WIDE)


QBIAS, VBIAS, EBIAS = 6, 7, 8
FIRST_COST = 1_000_000_000


def pack_body(*refs):
    weights, vectors, biases = refs[:3], refs[3:9], refs[9:12]
    message, lines = refs[12:]
    ways = lax.axis_size("fsdp")
    mine = lax.axis_index("fsdp")
    share, columns = weights[0].shape
    lines[...] = jnp.zeros_like(lines)
    for n, ref in enumerate(vectors):
        lines[n : n + 1, :share] = ref[...].reshape(1, -1).astype(WIDE)
    for n, ref in zip((QBIAS, VBIAS, EBIAS), biases):
        groups, size = ref.shape
        each = size * ways
        row = lax.broadcasted_iota(jnp.int32, (size, groups * each), 0)
        column = lax.broadcasted_iota(jnp.int32, (size, groups * each), 1)
        within = column
        for g in range(1, groups):
            within = jnp.where(column >= g * each, column - g * each, within)
        tiled = dot(ref[...], (within == row + mine * size).astype(LOW))
        group = lax.broadcasted_iota(jnp.int32, tiled.shape, 0)
        column = lax.broadcasted_iota(jnp.int32, tiled.shape, 1)
        keep = (column >= group * each) & (column < (group + 1) * each)
        flat = jnp.sum(jnp.where(keep, tiled, 0.0), 0, keepdims=True)
        for at in range(0, groups * each, share):
            part = flat[:, at : at + share]
            lines[n + at // share : n + at // share + 1, : part.shape[1]] = part
    message[share:, :] = lines[...].astype(LOW)
    for n, w in enumerate(weights):
        message[:share, n * columns : (n + 1) * columns] = w[...]


def merge(own, got, out):
    share = out.shape[1] // 2
    out[...] = jnp.zeros_like(out)
    mine, theirs = own[...], got[got.shape[0] - own.shape[0] :, :].astype(WIDE)
    out[:QBIAS, :share] = mine[:QBIAS, :share]
    out[:QBIAS, share:] = theirs[:QBIAS, :share]
    both = mine + theirs
    out[QBIAS : EBIAS + 1, :share] = both[QBIAS : EBIAS + 1, :share]
    out[EBIAS : EBIAS + 1, share:] = both[EBIAS + 1 : EBIAS + 2, :share]


def normed_rows(values):
    center = values - jnp.mean(values, -1, keepdims=True)
    return center * lax.rsqrt(jnp.mean(center * center, -1, keepdims=True) + EPS)


def norm_back_rows(values, gain, upstream):
    center = values - jnp.mean(values, -1, keepdims=True)
    spread = lax.rsqrt(jnp.mean(center * center, -1, keepdims=True) + EPS)
    xhat = center * spread
    z = upstream * gain
    grad = spread * (
        z - jnp.mean(z, -1, keepdims=True) - xhat * jnp.mean(z * xhat, -1, keepdims=True)
    )
    return grad, xhat


def third_of(message, n, size, features):
    return message[:size, n * features : (n + 1) * features]


def key_bias(count, shape, axis, seq):
    step = lax.broadcasted_iota(jnp.int32, shape, axis)
    place = lax.axis_index("context")
    core = lax.axis_index("tensor") & 1
    half = seq // 2
    position = step
    for b in range(shape[axis] // half):
        start = (place ^ (b // 2)) * seq + (core ^ (b % 2)) * half
        position = jnp.where(step >= b * half, step + (start - b * half), position)
    return jnp.where(position < count[0], 0.0, -1e30).astype(WIDE)


def head_mask(shape, head, head_dim):
    lane = lax.broadcasted_iota(jnp.int32, shape, 1)
    return (lane >= head * head_dim) & (lane < (head + 1) * head_dim)


def attend_rows(heads, head_dim, start, rows, qkv, bias):
    features = heads * head_dim
    q = qkv[start : start + rows, :features]
    k = qkv[:, features : 2 * features]
    v = qkv[:, 2 * features :]
    scale = head_dim**-0.5
    total = jnp.zeros((rows, features), WIDE)
    for h in range(heads):
        mine = head_mask(q.shape, h, head_dim)
        scores = dot_rt(jnp.where(mine, q, jnp.zeros_like(q)), k) * scale + bias
        raw = jnp.exp(scores - jnp.max(scores, -1, keepdims=True))
        got = dot(raw.astype(LOW), v) / jnp.sum(raw, -1, keepdims=True)
        total = jnp.where(mine, got, total)
    return total.astype(LOW)


def first_body(heads, head_dim, blocks, ways, count, *refs):
    pieces, refs = refs[:blocks], refs[blocks:]
    packed, lines, refs = refs[:ways], refs[ways], refs[ways + 1 :]
    vec, xhat, normed, qkv, context = refs
    rows = pieces[0].shape[0] // 2
    if ways == 2:
        merge(lines, packed[1], vec)
    else:
        vec[...] = lines[...]
    features = heads * head_dim
    for n, piece in enumerate(pieces):
        part = normed_rows(piece[:rows, :].astype(WIDE))
        xhat[n * rows : (n + 1) * rows, :] = part.astype(LOW)
        normed[n * rows : (n + 1) * rows, :] = (part * vec[0:1, :] + vec[1:2, :]).astype(LOW)
    size = normed.shape[1] // ways
    for n, row in enumerate((QBIAS, None, VBIAS)):
        got = sum(
            dot(normed[:, i * size : (i + 1) * size], third_of(w, n, size, features))
            for i, w in enumerate(packed)
        )
        if row is not None:
            got = got + vec[row : row + 1, :features]
        qkv[:, n * features : (n + 1) * features] = got.astype(LOW)
    bias = key_bias(count, (1, blocks * rows), 1, 2 * rows)
    context[...] = attend_rows(heads, head_dim, 0, 2 * rows, qkv, bias)


def out_body(ways, *refs):
    context, weights, (keep, send) = refs[0], refs[1 : 1 + ways], refs[1 + ways :]
    rows, size = keep.shape[0], keep.shape[1] // ways
    for i, w in enumerate(weights):
        part = dot(context[...], w[...]).astype(LOW)
        keep[:, i * size : (i + 1) * size] = part[:rows]
        send[:, i * size : (i + 1) * size] = part[rows:]


def rest_body(heads, head_dim, start, count, qkv, out):
    bias = key_bias(count, (1, qkv.shape[0]), 1, start)
    out[...] = attend_rows(heads, head_dim, start, out.shape[0], qkv, bias)


def second_body(tokens, near, far, vec, hidden, normed):
    total = tokens[: near.shape[0], :].astype(WIDE) + (near[...].astype(WIDE) + far[...].astype(WIDE))
    total = total + vec[2:3, :]
    hidden[...] = total
    normed[...] = (normed_rows(total) * vec[3:4, :] + vec[4:5, :]).astype(LOW)


def forward_body(blocks, ways, *refs):
    normed, cots, refs = refs[:blocks], refs[blocks : 2 * blocks], refs[2 * blocks :]
    vec, expand, reduce = refs[0], refs[1 : 1 + ways], refs[1 + ways : 1 + 2 * ways]
    normed_all, cot_all, act, grad, keep, send, out_keep, out_send, unit_sum, cot_sum, *aways = refs[
        1 + 2 * ways :
    ]
    rows = normed[0].shape[0]
    size = normed_all.shape[1] // ways
    units = act.shape[1]
    place = lax.axis_index("context")
    for n in range(blocks):
        normed_all[n * rows : (n + 1) * rows, :] = normed[n][...]
    for n in range(blocks):
        cot_all[n * rows : (n + 1) * rows, :] = cots[n][rows:, :]
    cot_sum[...] = jnp.sum(cot_all[...].astype(WIDE), 0, keepdims=True)
    step = min(256, units, size)
    back = [jnp.zeros((2 * rows, size), WIDE) for _ in range(ways)]
    out = [jnp.zeros((2 * rows, size), WIDE) for _ in range(ways)]
    for at in range(0, units, step):
        columns = slice(at, at + step)
        expands = [w[:, columns] for w in expand]
        reduces = [w[columns, :] for w in reduce]
        sides = [slice(i * size, (i + 1) * size) for i in range(ways)]
        value = sum(dot(normed_all[:, c], w) for c, w in zip(sides, expands))
        value = value + vec[EBIAS : EBIAS + 1, columns]
        cdf = 0.5 * (1.0 + lax.erf(value * (2.0**-0.5)))
        act[:, columns] = (value * cdf).astype(LOW)
        slope = cdf + value * jnp.exp(-0.5 * value * value) * 0.3989422804014327
        part = sum(dot_rt(cot_all[:, c], w) for c, w in zip(sides, reduces))
        part = (part * slope).astype(LOW)
        grad[:, columns] = part
        unit_sum[0:1, columns] = jnp.sum(part.astype(WIDE), 0, keepdims=True)
        own = act[: 2 * rows, columns]
        for i in range(ways):
            back[i] = back[i] + dot_rt(part[: 2 * rows], expands[i])
            out[i] = out[i] + dot(own, reduces[i])
    for i, c in enumerate(sides):
        keep[:, c] = back[i][:rows].astype(LOW)
        send[:, c] = back[i][rows:].astype(LOW)
        out_keep[:, c] = out[i][:rows].astype(LOW)
        out_send[:, c] = out[i][rows:].astype(LOW)
    if aways:
        many = units // 2
        chosen = pl.ds(pl.multiple_of((place & 1) * many, many), many)
        aways[0][...] = dot_lt(act[:, chosen], cot_all[:, size:]).astype(LOW)
        aways[1][...] = dot_lt(normed_all[:, size:], grad[...]).astype(LOW)


def second_back_body(near, far, hidden, cot, vec, grad_hidden, grad_branch):
    upstream = near[...].astype(WIDE) + far[...].astype(WIDE)
    grad, xhat = norm_back_rows(hidden[...], vec[3:4, :], upstream)
    total = grad + cot[grad.shape[0] :, :].astype(WIDE)
    grad_hidden[...] = total
    rows = total.shape[0]
    grad_branch[:rows, :] = total.astype(LOW)
    below = jnp.zeros((grad_branch.shape[0] - rows, total.shape[1]), WIDE)
    line = lax.broadcasted_iota(jnp.int32, below.shape, 0)
    below = jnp.where(line == 0, jnp.sum(upstream * xhat, 0, keepdims=True), below)
    below = jnp.where(line == 1, jnp.sum(upstream, 0, keepdims=True), below)
    grad_branch[rows:, :] = below.astype(LOW)


def attend_back_body(heads, head_dim, blocks, ways, count, *refs):
    pieces, refs = refs[:blocks], refs[blocks:]
    outs, qkv, packed = refs[:ways], refs[ways], refs[ways + 1 : 2 * ways + 1]
    normed, contexts = refs[2 * ways + 1], refs[2 * ways + 2 : 2 * ways + 4]
    branch, grad_qkv, keep, send, sums, norm_sums, head_sums, away = refs[2 * ways + 4 :]
    rows = keep.shape[0]
    features = heads * head_dim
    below = jnp.zeros((pieces[0].shape[0] - rows, branch.shape[1]), WIDE)
    for n, piece in enumerate(pieces):
        branch[n * rows : (n + 1) * rows, :] = piece[:rows, :]
        below = below + piece[rows:, :].astype(WIDE)
    norm_sums[...] = below[:2]
    size = branch.shape[1] // ways
    g = sum(
        dot_rt(branch[:, i * size : (i + 1) * size], w[...]) for i, w in enumerate(outs)
    ).astype(LOW)
    bias = key_bias(count, (branch.shape[0], 1), 0, 2 * rows)
    q = qkv[:, :features]
    k = qkv[:, features : 2 * features]
    v = qkv[:, 2 * features :]
    scale = head_dim**-0.5
    zero = jnp.zeros_like(q)
    totals = [jnp.zeros(q.shape, WIDE) for _ in range(3)]
    for h in range(heads):
        mine = head_mask(q.shape, h, head_dim)
        scores = dot_rt(k, jnp.where(mine, q, zero)) * scale + bias
        raw = jnp.exp(scores - jnp.max(scores, 0, keepdims=True))
        probs = raw * (1.0 / jnp.sum(raw, 0, keepdims=True))
        grad_probs = dot_rt(v, jnp.where(mine, g, zero))
        delta = jnp.sum(probs * grad_probs, 0, keepdims=True)
        grad_scores = (probs * (grad_probs - delta)).astype(LOW)
        totals[0] = jnp.where(mine, dot_lt(grad_scores, k) * scale, totals[0])
        totals[1] = jnp.where(mine, dot(grad_scores, q) * scale, totals[1])
        totals[2] = jnp.where(mine, dot(probs.astype(LOW), g), totals[2])
    for n in range(3):
        part = totals[n].astype(LOW)
        grad_qkv[:, n * features : (n + 1) * features] = part
        head_sums[0:1, n * features : (n + 1) * features] = jnp.sum(
            part.astype(WIDE), 0, keepdims=True
        )
    for i in range(ways):
        part = sum(
            dot_rt(
                grad_qkv[: 2 * rows, n * features : (n + 1) * features],
                third_of(packed[i], n, size, features),
            )
            for n in range(3)
        ).astype(LOW)
        keep[:, i * size : (i + 1) * size] = part[:rows]
        send[:, i * size : (i + 1) * size] = part[rows:]
    sums[...] = jnp.sum(branch[...].astype(WIDE), 0, keepdims=True)
    other = normed.shape[1] - away.shape[0]
    away[:, : 3 * features] = dot_lt(normed[:, other:], grad_qkv[...]).astype(LOW)
    first = contexts[0].shape[0]
    part = dot_lt(contexts[0][...], branch[:first, other:])
    part = (part + dot_lt(contexts[1][...], branch[first:, other:])).astype(LOW)
    for n in range(away.shape[0] // features):
        away[n * features : (n + 1) * features, 3 * features :] = part[
            :, n * features : (n + 1) * features
        ]


def first_sums_body(ways, grad_qkv, xhat, *refs):
    packed, out = refs[:ways], refs[ways]
    features = grad_qkv.shape[1] // 3
    size = xhat.shape[1] // ways
    for i in range(ways):
        part = sum(
            dot_rt(
                grad_qkv[:, n * features : (n + 1) * features],
                third_of(packed[i], n, size, features),
            )
            for n in range(3)
        )
        columns = slice(i * size, (i + 1) * size)
        out[0:1, columns] = jnp.sum(part * xhat[:, columns].astype(WIDE), 0, keepdims=True)
        out[1:2, columns] = jnp.sum(part, 0, keepdims=True)


def last_body(own, own_out, got, sums, plain, lines, *outs):
    query, key, value, out = outs[:4]
    vectors, (qbias, vbias, ebias) = outs[4:10], outs[10:]
    size = query.shape[1]
    for n, ref in enumerate((query, key, value)):
        columns = slice(n * size, (n + 1) * size)
        ref[...] = own[:, columns] + got[:, columns].astype(WIDE)
    for n in range(out.shape[1] // size):
        columns = slice(n * size, (n + 1) * size)
        out[:, columns] = own_out[:, columns] + got[columns, 3 * size :].astype(WIDE)
    count = len(vectors)
    total = sums[...] + lines[:count, :]
    for n, ref in enumerate(vectors):
        ref[...] = total[n : n + 1, :].reshape(ref.shape)
    heads, units = (
        plain[n : n + 1, :]
        + jnp.concatenate([lines[count + n : count + n + 1, :], lines[count + 2 + n : count + 3 + n, :]], 1)
        for n in range(2)
    )
    upper = lax.axis_index("fsdp") == 1
    for ref, row, start in ((qbias, heads, 0), (vbias, heads, 2 * size), (ebias, units, 0)):
        groups, half = ref.shape
        for g in range(groups):
            at = start + 2 * g * half
            ref[g : g + 1, :] = jnp.where(upper, row[:, at + half : at + 2 * half], row[:, at : at + half])


def first_back_body(near, far, tokens, grad_hidden, vec, out):
    upstream = near[...].astype(WIDE) + far[...].astype(WIDE)
    grad, _ = norm_back_rows(tokens[: near.shape[0], :].astype(WIDE), vec[0:1, :], upstream)
    out[...] = grad + grad_hidden[...]


def on_device(
    tokens,
    cotangent,
    valid_count,
    gain_first,
    shift_first,
    query_weight,
    query_bias,
    key_weight,
    value_weight,
    value_bias,
    output_weight,
    output_bias,
    gain_second,
    shift_second,
    expand_weight,
    expand_bias,
    reduce_weight,
    reduce_bias,
):
    images, seq, width = tokens.shape
    ways = lax.axis_size("fsdp")
    pair = ways == 2
    parts = 2 if pair else 1
    cycle = lax.axis_size("context")
    mine = lax.axis_index("fsdp")
    place = lax.axis_index("context")
    core = lax.axis_index("tensor") & 1
    share = gain_first.shape[0]
    heads = query_bias.shape[1]
    head_dim = query_bias.shape[0] * ways
    features = heads * head_dim
    units = expand_weight.shape[1]
    half = seq // 2
    blocks = 2 * cycle
    length = cycle * seq
    second = mine == 1

    def turned(value):
        if not pair:
            return value
        left, right = jnp.split(value, 2, -1)
        return jnp.where(second, jnp.concatenate([right, left], -1), value)

    def piece_of(value, which):
        return turned(lax.dynamic_slice_in_dim(value.reshape(seq, width), which * half, half, 0))

    def pieces_of(which):
        return jnp.concatenate([piece_of(tokens, which), piece_of(cotangent, which)], 0)

    own_piece = pieces_of(core)
    vectors = (gain_first, shift_first, output_bias, gain_second, shift_second, reduce_bias)
    biases = (query_bias, value_bias, expand_bias)
    thirds = (query_weight, key_weight, value_weight)

    if pair:
        across = lambda v: swap(v, "fsdp", 1)
        message, lines = kernel(
            pack_body,
            (low(share + 16, 3 * features), wide(16, 3 * features)),
            after(query_weight, own_piece),
            key_weight,
            value_weight,
            *vectors,
            *(b.T for b in biases),
            staged=True,
            limit=62,
        )
        first = across(message)
        packed = (message, first)
        output_parts = (output_weight, across(after(output_weight, message)))
        reduce_parts = (reduce_weight, across(after(reduce_weight, first)))
    else:
        gather = lambda v, axis=0: lax.all_gather(v, "fsdp", axis=axis, tiled=True)
        rows = [gather(v).reshape(1, -1) for v in vectors]
        rows += [gather(b).T.reshape(1, -1) for b in biases]
        lines = jnp.concatenate(
            [jnp.pad(r, ((0, 0), (0, width - r.shape[1]))) for r in rows]
            + [jnp.zeros((16 - len(rows), width), LOW)],
            0,
        ).astype(WIDE)
        packed = (jnp.concatenate([gather(w) for w in thirds], 1),)
        output_parts = (gather(output_weight, 1),)
        expand_parts = (gather(expand_weight),)
        reduce_parts = (gather(reduce_weight, 1),)

    mine_tokens = spread_context(own_piece)
    both_pieces = woven(
        mine_tokens,
        [pieces_of(1 - core)]
        + [swap(after(m, packed[-1]), "tensor", 1) for m in mine_tokens[1:]],
    )
    if pair:
        expand_parts = (expand_weight, across(after(expand_weight, mine_tokens[1])))

    vec, xhat_all, normed_all, qkv, context_own = kernel(
        lambda *refs: first_body(heads, head_dim, blocks, parts, *refs),
        (
            wide(16, width),
            low(length, width),
            low(length, width),
            low(length, 3 * features),
            low(seq, features),
        ),
        *both_pieces,
        *packed,
        lines,
        count=valid_count,
        flops=FIRST_COST,
    )
    keep, send = kernel(
        lambda *refs: out_body(parts, *refs),
        (low(half, width), low(half, width)),
        context_own,
        *output_parts,
    )
    near, far = last_terms(keep, send)
    context_rest = kernel(
        lambda *refs: rest_body(heads, head_dim, seq, *refs),
        low(length - seq, features),
        after(qkv, near),
        count=valid_count,
    )
    far = after(far, context_rest)
    hidden, normed_piece = kernel(
        second_body, (wide(half, width), low(half, width)), own_piece, near, far, vec
    )

    mine_normed = spread_context(normed_piece)
    theirs = [swap(m, "tensor", 1) for m in mine_normed[:1]]
    mine_normed[1:] = [after(m, expand_parts[-1]) for m in mine_normed[1:]]
    theirs += [swap(m, "tensor", 1) for m in mine_normed[1:]]
    (
        normed_two,
        cot_all,
        activated,
        grad_expanded,
        keep,
        send,
        out_keep,
        out_send,
        unit_sum,
        cot_sum,
        *aways,
    ) = kernel(
        lambda *refs: forward_body(blocks, parts, *refs),
        (low(length, width),) * 2
        + (low(length, units),) * 2
        + (low(half, width),) * 4
        + (wide(1, units), wide(1, width))
        + ((low(units // 2, share), low(share, units)) if pair else ()),
        *woven(mine_normed, theirs),
        *both_pieces,
        vec,
        *expand_parts,
        *reduce_parts,
        flops=10 * length * width * units,
        moved=12 * length * width,
        staged=True,
        limit=62,
    )
    near, far = last_terms(keep, send)
    if pair:
        many = units // 2
        act_half = lax.dynamic_slice_in_dim(activated, (place & 1) * many, many, 1)
        cot_own, normed_own = segments(cot_all, 2)[0], segments(normed_two, 2)[0]
    grad_hidden, grad_piece = kernel(
        second_back_body,
        (wide(half, width), low(half + 16, width)),
        near,
        far,
        hidden,
        own_piece,
        vec,
    )

    def scatter(value, axis):
        return lax.psum_scatter(value.astype(LOW), "fsdp", scatter_dimension=axis, tiled=True)

    def weight_grad(left, right, along):
        if not pair:
            return scatter(dot_lt(left, right), along).astype(WIDE)
        if along:
            own, other = segments(right, 2)
            away = across(dot_lt(left, other).astype(LOW))
            return pin(dot_lt(left, own)) + away.astype(WIDE)
        own, other = segments(left, 2)
        away = across(dot_lt(other, right).astype(LOW))
        return pin(dot_lt(own, right)) + away.astype(WIDE)

    if pair:
        reduce_got, expand_got = (across(a) for a in aways)

        def both_halves(value, theirs, axis):
            odd = (place & 1) != 0
            return jnp.concatenate(
                [jnp.where(odd, theirs, value), jnp.where(odd, value, theirs)], axis
            ).astype(WIDE)

    else:
        grad_reduce = weight_grad(activated, cot_all, 1)
        grad_expand = weight_grad(normed_two, grad_expanded, 0)

    mine_grads = spread_context(grad_piece)
    out_near, out_far = last_terms(after(out_keep, grad_piece), after(out_send, grad_piece))
    ready = [out_far]
    theirs = [swap(m, "tensor", 1) for m in mine_grads[:1]]
    if pair:
        reduce_half = pin((dot_lt(act_half, cot_own) + reduce_got.astype(WIDE)).astype(LOW))
        mine_grads[1:] = lax.optimization_barrier((*mine_grads[1:], reduce_got))[:-1]
        expand_own = pin(dot_lt(after(normed_own, grad_piece), grad_expanded))
        ready += [reduce_half, expand_own]
    theirs += [swap(m, "tensor", 1) for m in mine_grads[1:]]
    grad_branch, grad_qkv, keep, send, branch_sum, norm_sums, head_sum, away = kernel(
        lambda *refs: attend_back_body(heads, head_dim, blocks, parts, *refs),
        (
            low(length, width),
            low(length, 3 * features),
            low(half, width),
            low(half, width),
            wide(1, width),
            wide(2, width),
            wide(1, 3 * features),
            low(width // parts, 4 * features),
        ),
        *woven(mine_grads, theirs),
        *output_parts,
        after(qkv, *ready),
        *packed,
        normed_all,
        context_own,
        context_rest,
        count=valid_count,
        flops=10 * length * length * features,
        moved=8 * length * width,
    )
    if pair:
        qkv_got = across(away)
    if pair:
        send = after(send, expand_got)
    near, far = last_terms(keep, send)
    gn_far = far
    if pair:
        reduce_theirs = swap(reduce_half, "context", 1)
        grad_expand = expand_own + expand_got.astype(WIDE)
    grad_token_piece = kernel(
        first_back_body, wide(half, width), near, far, own_piece, grad_hidden, vec
    )

    def both_cores(value):
        theirs = swap(value, "tensor", 1)
        upper = core == 1
        return turned(
            jnp.concatenate([jnp.where(upper, theirs, value), jnp.where(upper, value, theirs)], 0)
        ).reshape(tokens.shape)

    grad_tokens = both_cores(grad_token_piece)

    reduced = out_near.astype(WIDE) + out_far.astype(WIDE) + vec[5:6, :]
    output = both_cores((hidden + reduced).astype(LOW))

    if not pair:
        grad_weights = scatter(dot_lt(normed_all, grad_qkv), 0).astype(WIDE)
        grad_query, grad_key, grad_value = jnp.split(grad_weights, 3, 1)
        context_all = jnp.concatenate([context_own, context_rest], 0)
        grad_output = scatter(dot_lt(context_all, grad_branch), 1).astype(WIDE)

    first_sums = kernel(
        lambda *refs: first_sums_body(parts, *refs), wide(2, width), after(grad_qkv, gn_far), xhat_all, *packed
    )
    bit = 1
    while bit < lax.axis_size("tensor"):
        first_sums = first_sums + swap(first_sums, "tensor", bit)
        bit *= 2
    if pair:
        grad_reduce = both_halves(reduce_half, after(reduce_theirs, gn_far), 0)
    sums = jnp.concatenate([first_sums, norm_sums, branch_sum, cot_sum], 0)
    plain = jnp.concatenate(
        [jnp.pad(head_sum, ((0, 0), (0, width - 3 * features))), unit_sum], 0
    )
    if pair:
        own, other = segments(sums, 2)
        lines = across(jnp.concatenate([other, *segments(plain, 2)], 0))
        grads = kernel(
            last_body,
            (wide(share, features),) * 3
            + (wide(features, share),)
            + (wide(share),) * 6
            + (wide(heads, head_dim // 2),) * 2
            + (wide(expand_bias.shape[1], expand_bias.shape[0]),),
            after(dot_lt(segments(after(normed_all, gn_far), 2)[0], grad_qkv), grad_tokens, output),
            dot_lt(
                jnp.concatenate([context_own, context_rest], 0),
                segments(after(grad_branch, gn_far), 2)[0],
            ),
            qkv_got,
            own,
            plain,
            lines,
        )
        grad_query, grad_key, grad_value, grad_output, *sums = grads[:10]
        grad_qbias, grad_vbias, grad_ebias = (g.T for g in grads[10:])
    else:
        sums = scatter(sums, 1).astype(WIDE)
        plain = lax.psum(plain, "fsdp")

        def own_rows(value):
            size = value.shape[0] // ways
            return lax.dynamic_slice_in_dim(value, mine * size, size, 0)

        grad_ebias = own_rows(plain[1].reshape(-1, expand_bias.shape[0] * ways).T)
        grad_qbias, grad_vbias = (
            own_rows(plain[0, n * features : (n + 1) * features].reshape(heads, head_dim).T)
            for n in (0, 2)
        )
    return (
        output,
        grad_tokens,
        sums[0],
        sums[1],
        grad_query,
        grad_qbias,
        grad_key,
        grad_value,
        grad_vbias,
        grad_output,
        sums[4],
        sums[2],
        sums[3],
        grad_expand,
        grad_ebias,
        grad_reduce,
        sums[5],
    )


def solution(mesh):
    rows = P("fsdp", "context", None)
    vector = P("fsdp")
    split = P("fsdp", "tensor")
    turned = P("tensor", "fsdp")
    in_specs = (rows, rows, vector, vector, vector, split, split, split, split, split)
    in_specs += (turned, vector, vector, vector, split, split, turned, vector)
    out_specs = (rows, rows, vector, vector, split, split, split, split, split)
    out_specs += (turned, vector, vector, vector, split, split, turned, vector)
    return jax.shard_map(
        on_device, mesh=mesh, in_specs=in_specs, out_specs=out_specs, check_vma=False
    )
```

```python
import jax
import jax.numpy as jnp
from jax import lax
from jax.experimental import pallas as pl
from jax.experimental.pallas import tpu as pltpu
from jax.sharding import PartitionSpec as P

EPS = 1e-06
LOW = jnp.bfloat16
WIDE = jnp.float32


def swap(block, axis, bit):
    return lax.ppermute(block, axis, [(i, i ^ bit) for i in range(lax.axis_size(axis))])


def after(value, *others):
    return lax.optimization_barrier((value, *others))[0]


def pin(value):
    return lax.optimization_barrier(value)


def dot(left, right):
    return lax.dot_general(left, right, (((1,), (0,)), ((), ())), preferred_element_type=WIDE)


def dot_rt(left, right):
    return lax.dot_general(left, right, (((1,), (1,)), ((), ())), preferred_element_type=WIDE)


def dot_lt(left, right):
    return lax.dot_general(left, right, (((0,), (0,)), ((), ())), preferred_element_type=WIDE)


def segments(value, count):
    size = value.shape[1] // count
    return [value[:, i * size : (i + 1) * size] for i in range(count)]


def sum_cores(keep, send):
    return (keep.astype(WIDE) + swap(send, "tensor", 1).astype(WIDE)).astype(LOW)


def last_terms(keep, send):
    value = pin(sum_cores(keep, send))
    bit = 2
    while True:
        got = swap(value, "tensor", bit)
        bit *= 2
        if bit >= lax.axis_size("tensor"):
            return value, got
        value = pin((value.astype(WIDE) + got.astype(WIDE)).astype(LOW))


def spread_context(piece):
    return [piece] + [swap(piece, "context", k) for k in range(1, lax.axis_size("context"))]


def woven(mine, theirs):
    return [block for both in zip(mine, theirs) for block in both]


class Late:
    def __init__(self, ref, copy):
        self.ref, self.copy, self.shape = ref, copy, ref.shape

    def wait(self):
        if self.copy is not None:
            self.copy.wait()
            self.copy = None

    def __getitem__(self, index):
        self.wait()
        return self.ref[index]


def kernel(body, out_shape, *args, count=None, flops=0, moved=0, staged=False, limit=48):
    scalars = [] if count is None else [count]
    first, last = len(scalars), len(scalars) + len(args)

    def run(*refs):
        buffers, arrived = refs[-len(args) - 1 : -1], refs[-1]
        inputs = []
        for n, (source, buffer) in enumerate(zip(refs[first:last], buffers)):
            copy = pltpu.make_async_copy(source, buffer, arrived.at[n])
            copy.start()
            inputs.append(Late(buffer, copy))
        body(*refs[:first], *inputs, *refs[last : -len(args) - 1])
        for late in inputs:
            late.wait()

    scratch = [pltpu.VMEM(a.shape, a.dtype) for a in args] + [pltpu.SemaphoreType.DMA((len(args),))]
    space = pltpu.HBM if staged else pltpu.VMEM
    return pl.pallas_call(
        run if staged else body,
        out_shape=out_shape,
        in_specs=[pl.BlockSpec(memory_space=pltpu.SMEM)] * first
        + [pl.BlockSpec(memory_space=space)] * len(args),
        scratch_shapes=scratch if staged else (),
        compiler_params=pltpu.CompilerParams(vmem_limit_bytes=limit << 20),
        cost_estimate=pl.CostEstimate(flops=flops, bytes_accessed=moved, transcendentals=0),
    )(*scalars, *args)


def low(*shape):
    return jax.ShapeDtypeStruct(shape, LOW)


def wide(*shape):
    return jax.ShapeDtypeStruct(shape, WIDE)


QBIAS, VBIAS, EBIAS = 6, 7, 8
FIRST_COST = 1_000_000_000


def pack_body(*refs):
    weights, vectors, biases = refs[:3], refs[3:9], refs[9:12]
    message, lines = refs[12:]
    ways = lax.axis_size("fsdp")
    mine = lax.axis_index("fsdp")
    share, columns = weights[0].shape
    lines[...] = jnp.zeros_like(lines)
    for n, ref in enumerate(vectors):
        lines[n : n + 1, :share] = ref[...].reshape(1, -1).astype(WIDE)
    for n, ref in zip((QBIAS, VBIAS, EBIAS), biases):
        groups, size = ref.shape
        each = size * ways
        row = lax.broadcasted_iota(jnp.int32, (size, groups * each), 0)
        column = lax.broadcasted_iota(jnp.int32, (size, groups * each), 1)
        within = column
        for g in range(1, groups):
            within = jnp.where(column >= g * each, column - g * each, within)
        tiled = dot(ref[...], (within == row + mine * size).astype(LOW))
        group = lax.broadcasted_iota(jnp.int32, tiled.shape, 0)
        column = lax.broadcasted_iota(jnp.int32, tiled.shape, 1)
        keep = (column >= group * each) & (column < (group + 1) * each)
        flat = jnp.sum(jnp.where(keep, tiled, 0.0), 0, keepdims=True)
        for at in range(0, groups * each, share):
            part = flat[:, at : at + share]
            lines[n + at // share : n + at // share + 1, : part.shape[1]] = part
    message[share:, :] = lines[...].astype(LOW)
    for n, w in enumerate(weights):
        message[:share, n * columns : (n + 1) * columns] = w[...]


def merge(own, got, out):
    share = out.shape[1] // 2
    out[...] = jnp.zeros_like(out)
    mine, theirs = own[...], got[got.shape[0] - own.shape[0] :, :].astype(WIDE)
    out[:QBIAS, :share] = mine[:QBIAS, :share]
    out[:QBIAS, share:] = theirs[:QBIAS, :share]
    both = mine + theirs
    out[QBIAS : EBIAS + 1, :share] = both[QBIAS : EBIAS + 1, :share]
    out[EBIAS : EBIAS + 1, share:] = both[EBIAS + 1 : EBIAS + 2, :share]


def normed_rows(values):
    center = values - jnp.mean(values, -1, keepdims=True)
    return center * lax.rsqrt(jnp.mean(center * center, -1, keepdims=True) + EPS)


def norm_back_rows(values, gain, upstream):
    center = values - jnp.mean(values, -1, keepdims=True)
    spread = lax.rsqrt(jnp.mean(center * center, -1, keepdims=True) + EPS)
    xhat = center * spread
    z = upstream * gain
    grad = spread * (
        z - jnp.mean(z, -1, keepdims=True) - xhat * jnp.mean(z * xhat, -1, keepdims=True)
    )
    return grad, xhat


def third_of(message, n, size, features):
    return message[:size, n * features : (n + 1) * features]


def key_bias(count, shape, axis, seq):
    step = lax.broadcasted_iota(jnp.int32, shape, axis)
    place = lax.axis_index("context")
    core = lax.axis_index("tensor") & 1
    half = seq // 2
    position = step
    for b in range(shape[axis] // half):
        start = (place ^ (b // 2)) * seq + (core ^ (b % 2)) * half
        position = jnp.where(step >= b * half, step + (start - b * half), position)
    return jnp.where(position < count[0], 0.0, -1e30).astype(WIDE)


def head_mask(shape, head, head_dim):
    lane = lax.broadcasted_iota(jnp.int32, shape, 1)
    return (lane >= head * head_dim) & (lane < (head + 1) * head_dim)


def attend_rows(heads, head_dim, start, rows, qkv, bias):
    features = heads * head_dim
    q = qkv[start : start + rows, :features]
    k = qkv[:, features : 2 * features]
    v = qkv[:, 2 * features :]
    scale = head_dim**-0.5
    total = jnp.zeros((rows, features), WIDE)
    for h in range(heads):
        mine = head_mask(q.shape, h, head_dim)
        scores = dot_rt(jnp.where(mine, q, jnp.zeros_like(q)), k) * scale + bias
        raw = jnp.exp(scores - jnp.max(scores, -1, keepdims=True))
        got = dot(raw.astype(LOW), v) / jnp.sum(raw, -1, keepdims=True)
        total = jnp.where(mine, got, total)
    return total.astype(LOW)


def first_body(heads, head_dim, blocks, ways, count, *refs):
    pieces, refs = refs[:blocks], refs[blocks:]
    packed, lines, refs = refs[:ways], refs[ways], refs[ways + 1 :]
    vec, xhat, normed, qkv, context = refs
    rows = pieces[0].shape[0] // 2
    if ways == 2:
        merge(lines, packed[1], vec)
    else:
        vec[...] = lines[...]
    features = heads * head_dim
    for n, piece in enumerate(pieces):
        part = normed_rows(piece[:rows, :].astype(WIDE))
        xhat[n * rows : (n + 1) * rows, :] = part.astype(LOW)
        normed[n * rows : (n + 1) * rows, :] = (part * vec[0:1, :] + vec[1:2, :]).astype(LOW)
    size = normed.shape[1] // ways
    for n, row in enumerate((QBIAS, None, VBIAS)):
        got = sum(
            dot(normed[:, i * size : (i + 1) * size], third_of(w, n, size, features))
            for i, w in enumerate(packed)
        )
        if row is not None:
            got = got + vec[row : row + 1, :features]
        qkv[:, n * features : (n + 1) * features] = got.astype(LOW)
    bias = key_bias(count, (1, blocks * rows), 1, 2 * rows)
    context[...] = attend_rows(heads, head_dim, 0, 2 * rows, qkv, bias)


def out_body(ways, *refs):
    context, weights, (keep, send) = refs[0], refs[1 : 1 + ways], refs[1 + ways :]
    rows, size = keep.shape[0], keep.shape[1] // ways
    for i, w in enumerate(weights):
        part = dot(context[...], w[...]).astype(LOW)
        keep[:, i * size : (i + 1) * size] = part[:rows]
        send[:, i * size : (i + 1) * size] = part[rows:]


def rest_body(heads, head_dim, start, count, qkv, out):
    bias = key_bias(count, (1, qkv.shape[0]), 1, start)
    out[...] = attend_rows(heads, head_dim, start, out.shape[0], qkv, bias)


def second_body(tokens, near, far, vec, hidden, normed):
    total = tokens[: near.shape[0], :].astype(WIDE) + (near[...].astype(WIDE) + far[...].astype(WIDE))
    total = total + vec[2:3, :]
    hidden[...] = total
    normed[...] = (normed_rows(total) * vec[3:4, :] + vec[4:5, :]).astype(LOW)


def forward_body(blocks, ways, *refs):
    normed, vec, expand, refs = refs[:blocks], refs[blocks], refs[blocks + 1 :][:ways], refs[blocks + 1 + ways :]
    cots, reduce, refs = refs[:blocks], refs[blocks : blocks + ways], refs[blocks + ways :]
    normed_all, cot_all, act, grad, keep, send, out_keep, out_send, unit_sum, cot_sum, *aways = refs
    rows = normed[0].shape[0]
    size = normed_all.shape[1] // ways
    units = act.shape[1]
    place = lax.axis_index("context")
    for n in range(blocks):
        normed_all[n * rows : (n + 1) * rows, :] = normed[n][...]
    step = min(256, units, size)
    back = [jnp.zeros((2 * rows, size), WIDE) for _ in range(ways)]
    out = [jnp.zeros((2 * rows, size), WIDE) for _ in range(ways)]
    for at in range(0, units, step):
        columns = slice(at, at + step)
        expands = [w[:, columns] for w in expand]
        sides = [slice(i * size, (i + 1) * size) for i in range(ways)]
        value = sum(dot(normed_all[:, c], w) for c, w in zip(sides, expands))
        value = value + vec[EBIAS : EBIAS + 1, columns]
        cdf = 0.5 * (1.0 + lax.erf(value * (2.0**-0.5)))
        act[:, columns] = (value * cdf).astype(LOW)
        slope = cdf + value * jnp.exp(-0.5 * value * value) * 0.3989422804014327
        if at == 0:
            for n in range(blocks):
                cot_all[n * rows : (n + 1) * rows, :] = cots[n][rows:, :]
            cot_sum[...] = jnp.sum(cot_all[...].astype(WIDE), 0, keepdims=True)
        reduces = [w[columns, :] for w in reduce]
        part = sum(dot_rt(cot_all[:, c], w) for c, w in zip(sides, reduces))
        part = (part * slope).astype(LOW)
        grad[:, columns] = part
        unit_sum[0:1, columns] = jnp.sum(part.astype(WIDE), 0, keepdims=True)
        own = act[: 2 * rows, columns]
        for i in range(ways):
            back[i] = back[i] + dot_rt(part[: 2 * rows], expands[i])
            out[i] = out[i] + dot(own, reduces[i])
    for i, c in enumerate(sides):
        keep[:, c] = back[i][:rows].astype(LOW)
        send[:, c] = back[i][rows:].astype(LOW)
        out_keep[:, c] = out[i][:rows].astype(LOW)
        out_send[:, c] = out[i][rows:].astype(LOW)
    if aways:
        many = units // 2
        chosen = pl.ds(pl.multiple_of((place & 1) * many, many), many)
        aways[0][...] = dot_lt(act[:, chosen], cot_all[:, size:]).astype(LOW)
        aways[1][...] = dot_lt(normed_all[:, size:], grad[...]).astype(LOW)


def second_back_body(near, far, hidden, cot, vec, grad_hidden, grad_branch):
    upstream = near[...].astype(WIDE) + far[...].astype(WIDE)
    grad, xhat = norm_back_rows(hidden[...], vec[3:4, :], upstream)
    total = grad + cot[grad.shape[0] :, :].astype(WIDE)
    grad_hidden[...] = total
    rows = total.shape[0]
    grad_branch[:rows, :] = total.astype(LOW)
    below = jnp.zeros((grad_branch.shape[0] - rows, total.shape[1]), WIDE)
    line = lax.broadcasted_iota(jnp.int32, below.shape, 0)
    below = jnp.where(line == 0, jnp.sum(upstream * xhat, 0, keepdims=True), below)
    below = jnp.where(line == 1, jnp.sum(upstream, 0, keepdims=True), below)
    grad_branch[rows:, :] = below.astype(LOW)


def attend_back_body(heads, head_dim, blocks, ways, count, *refs):
    pieces, refs = refs[:blocks], refs[blocks:]
    outs, qkv, packed = refs[:ways], refs[ways], refs[ways + 1 : 2 * ways + 1]
    normed, contexts = refs[2 * ways + 1], refs[2 * ways + 2 : 2 * ways + 4]
    branch, grad_qkv, keep, send, sums, norm_sums, head_sums, away = refs[2 * ways + 4 :]
    rows = keep.shape[0]
    features = heads * head_dim
    below = jnp.zeros((pieces[0].shape[0] - rows, branch.shape[1]), WIDE)
    for n, piece in enumerate(pieces):
        branch[n * rows : (n + 1) * rows, :] = piece[:rows, :]
        below = below + piece[rows:, :].astype(WIDE)
    norm_sums[...] = below[:2]
    size = branch.shape[1] // ways
    g = sum(
        dot_rt(branch[:, i * size : (i + 1) * size], w[...]) for i, w in enumerate(outs)
    ).astype(LOW)
    bias = key_bias(count, (branch.shape[0], 1), 0, 2 * rows)
    q = qkv[:, :features]
    k = qkv[:, features : 2 * features]
    v = qkv[:, 2 * features :]
    scale = head_dim**-0.5
    zero = jnp.zeros_like(q)
    totals = [jnp.zeros(q.shape, WIDE) for _ in range(3)]
    for h in range(heads):
        mine = head_mask(q.shape, h, head_dim)
        scores = dot_rt(k, jnp.where(mine, q, zero)) * scale + bias
        raw = jnp.exp(scores - jnp.max(scores, 0, keepdims=True))
        probs = raw * (1.0 / jnp.sum(raw, 0, keepdims=True))
        grad_probs = dot_rt(v, jnp.where(mine, g, zero))
        delta = jnp.sum(probs * grad_probs, 0, keepdims=True)
        grad_scores = (probs * (grad_probs - delta)).astype(LOW)
        totals[0] = jnp.where(mine, dot_lt(grad_scores, k) * scale, totals[0])
        totals[1] = jnp.where(mine, dot(grad_scores, q) * scale, totals[1])
        totals[2] = jnp.where(mine, dot(probs.astype(LOW), g), totals[2])
    for n in range(3):
        part = totals[n].astype(LOW)
        grad_qkv[:, n * features : (n + 1) * features] = part
        head_sums[0:1, n * features : (n + 1) * features] = jnp.sum(
            part.astype(WIDE), 0, keepdims=True
        )
    for i in range(ways):
        part = sum(
            dot_rt(
                grad_qkv[: 2 * rows, n * features : (n + 1) * features],
                third_of(packed[i], n, size, features),
            )
            for n in range(3)
        ).astype(LOW)
        keep[:, i * size : (i + 1) * size] = part[:rows]
        send[:, i * size : (i + 1) * size] = part[rows:]
    sums[...] = jnp.sum(branch[...].astype(WIDE), 0, keepdims=True)
    other = normed.shape[1] - away.shape[0]
    away[:, : 3 * features] = dot_lt(normed[:, other:], grad_qkv[...]).astype(LOW)
    first = contexts[0].shape[0]
    part = dot_lt(contexts[0][...], branch[:first, other:])
    part = (part + dot_lt(contexts[1][...], branch[first:, other:])).astype(LOW)
    for n in range(away.shape[0] // features):
        away[n * features : (n + 1) * features, 3 * features :] = part[
            :, n * features : (n + 1) * features
        ]


def first_sums_body(ways, grad_qkv, xhat, *refs):
    packed, out = refs[:ways], refs[ways]
    features = grad_qkv.shape[1] // 3
    size = xhat.shape[1] // ways
    for i in range(ways):
        part = sum(
            dot_rt(
                grad_qkv[:, n * features : (n + 1) * features],
                third_of(packed[i], n, size, features),
            )
            for n in range(3)
        )
        columns = slice(i * size, (i + 1) * size)
        out[0:1, columns] = jnp.sum(part * xhat[:, columns].astype(WIDE), 0, keepdims=True)
        out[1:2, columns] = jnp.sum(part, 0, keepdims=True)


def last_body(own, own_out, got, sums, plain, lines, *outs):
    query, key, value, out = outs[:4]
    vectors, (qbias, vbias, ebias) = outs[4:10], outs[10:]
    size = query.shape[1]
    for n, ref in enumerate((query, key, value)):
        columns = slice(n * size, (n + 1) * size)
        ref[...] = own[:, columns] + got[:, columns].astype(WIDE)
    for n in range(out.shape[1] // size):
        columns = slice(n * size, (n + 1) * size)
        out[:, columns] = own_out[:, columns] + got[columns, 3 * size :].astype(WIDE)
    count = len(vectors)
    total = sums[...] + lines[:count, :]
    for n, ref in enumerate(vectors):
        ref[...] = total[n : n + 1, :].reshape(ref.shape)
    heads, units = (
        plain[n : n + 1, :]
        + jnp.concatenate([lines[count + n : count + n + 1, :], lines[count + 2 + n : count + 3 + n, :]], 1)
        for n in range(2)
    )
    upper = lax.axis_index("fsdp") == 1
    for ref, row, start in ((qbias, heads, 0), (vbias, heads, 2 * size), (ebias, units, 0)):
        groups, half = ref.shape
        for g in range(groups):
            at = start + 2 * g * half
            ref[g : g + 1, :] = jnp.where(upper, row[:, at + half : at + 2 * half], row[:, at : at + half])


def first_back_body(near, far, tokens, grad_hidden, vec, out):
    upstream = near[...].astype(WIDE) + far[...].astype(WIDE)
    grad, _ = norm_back_rows(tokens[: near.shape[0], :].astype(WIDE), vec[0:1, :], upstream)
    out[...] = grad + grad_hidden[...]


def on_device(
    tokens,
    cotangent,
    valid_count,
    gain_first,
    shift_first,
    query_weight,
    query_bias,
    key_weight,
    value_weight,
    value_bias,
    output_weight,
    output_bias,
    gain_second,
    shift_second,
    expand_weight,
    expand_bias,
    reduce_weight,
    reduce_bias,
):
    images, seq, width = tokens.shape
    ways = lax.axis_size("fsdp")
    pair = ways == 2
    parts = 2 if pair else 1
    cycle = lax.axis_size("context")
    mine = lax.axis_index("fsdp")
    place = lax.axis_index("context")
    core = lax.axis_index("tensor") & 1
    share = gain_first.shape[0]
    heads = query_bias.shape[1]
    head_dim = query_bias.shape[0] * ways
    features = heads * head_dim
    units = expand_weight.shape[1]
    half = seq // 2
    blocks = 2 * cycle
    length = cycle * seq
    second = mine == 1

    def turned(value):
        if not pair:
            return value
        left, right = jnp.split(value, 2, -1)
        return jnp.where(second, jnp.concatenate([right, left], -1), value)

    def piece_of(value, which):
        return turned(lax.dynamic_slice_in_dim(value.reshape(seq, width), which * half, half, 0))

    def pieces_of(which):
        return jnp.concatenate([piece_of(tokens, which), piece_of(cotangent, which)], 0)

    own_piece = pieces_of(core)
    vectors = (gain_first, shift_first, output_bias, gain_second, shift_second, reduce_bias)
    biases = (query_bias, value_bias, expand_bias)
    thirds = (query_weight, key_weight, value_weight)

    if pair:
        across = lambda v: swap(v, "fsdp", 1)
        message, lines = kernel(
            pack_body,
            (low(share + 16, 3 * features), wide(16, 3 * features)),
            query_weight,
            key_weight,
            value_weight,
            *vectors,
            *(b.T for b in biases),
            staged=True,
            limit=62,
        )
        first = across(message)
        packed = (message, first)
        output_parts = (output_weight, across(after(output_weight, message)))
        reduce_parts = (reduce_weight, across(after(reduce_weight, first)))
    else:
        gather = lambda v, axis=0: lax.all_gather(v, "fsdp", axis=axis, tiled=True)
        rows = [gather(v).reshape(1, -1) for v in vectors]
        rows += [gather(b).T.reshape(1, -1) for b in biases]
        lines = jnp.concatenate(
            [jnp.pad(r, ((0, 0), (0, width - r.shape[1]))) for r in rows]
            + [jnp.zeros((16 - len(rows), width), LOW)],
            0,
        ).astype(WIDE)
        packed = (jnp.concatenate([gather(w) for w in thirds], 1),)
        output_parts = (gather(output_weight, 1),)
        expand_parts = (gather(expand_weight),)
        reduce_parts = (gather(reduce_weight, 1),)

    mine_tokens = spread_context(own_piece)
    both_pieces = woven(
        mine_tokens,
        [pieces_of(1 - core)]
        + [swap(after(m, packed[-1]), "tensor", 1) for m in mine_tokens[1:]],
    )
    if pair:
        expand_parts = (expand_weight, across(after(expand_weight, mine_tokens[1])))

    vec, xhat_all, normed_all, qkv, context_own = kernel(
        lambda *refs: first_body(heads, head_dim, blocks, parts, *refs),
        (
            wide(16, width),
            low(length, width),
            low(length, width),
            low(length, 3 * features),
            low(seq, features),
        ),
        *both_pieces,
        *packed,
        lines,
        count=valid_count,
        flops=FIRST_COST,
    )
    keep, send = kernel(
        lambda *refs: out_body(parts, *refs),
        (low(half, width), low(half, width)),
        context_own,
        *output_parts,
    )
    near, far = last_terms(keep, send)
    context_rest = kernel(
        lambda *refs: rest_body(heads, head_dim, seq, *refs),
        low(length - seq, features),
        after(qkv, near),
        count=valid_count,
    )
    far = after(far, context_rest)
    hidden, normed_piece = kernel(
        second_body, (wide(half, width), low(half, width)), own_piece, near, far, vec
    )

    mine_normed = spread_context(normed_piece)
    theirs = [swap(m, "tensor", 1) for m in mine_normed[:1]]
    mine_normed[1:] = [after(m, expand_parts[-1]) for m in mine_normed[1:]]
    theirs += [swap(m, "tensor", 1) for m in mine_normed[1:]]
    (
        normed_two,
        cot_all,
        activated,
        grad_expanded,
        keep,
        send,
        out_keep,
        out_send,
        unit_sum,
        cot_sum,
        *aways,
    ) = kernel(
        lambda *refs: forward_body(blocks, parts, *refs),
        (low(length, width),) * 2
        + (low(length, units),) * 2
        + (low(half, width),) * 4
        + (wide(1, units), wide(1, width))
        + ((low(units // 2, share), low(share, units)) if pair else ()),
        *woven(mine_normed, theirs),
        vec,
        *expand_parts,
        *both_pieces,
        *reduce_parts,
        flops=10 * length * width * units,
        moved=12 * length * width,
        staged=True,
        limit=62,
    )
    near, far = last_terms(keep, send)
    if pair:
        many = units // 2
        act_half = lax.dynamic_slice_in_dim(activated, (place & 1) * many, many, 1)
        cot_own, normed_own = segments(cot_all, 2)[0], segments(normed_two, 2)[0]
    grad_hidden, grad_piece = kernel(
        second_back_body,
        (wide(half, width), low(half + 16, width)),
        near,
        far,
        hidden,
        own_piece,
        vec,
    )

    def scatter(value, axis):
        return lax.psum_scatter(value.astype(LOW), "fsdp", scatter_dimension=axis, tiled=True)

    def weight_grad(left, right, along):
        if not pair:
            return scatter(dot_lt(left, right), along).astype(WIDE)
        if along:
            own, other = segments(right, 2)
            away = across(dot_lt(left, other).astype(LOW))
            return pin(dot_lt(left, own)) + away.astype(WIDE)
        own, other = segments(left, 2)
        away = across(dot_lt(other, right).astype(LOW))
        return pin(dot_lt(own, right)) + away.astype(WIDE)

    if pair:
        reduce_got, expand_got = (across(a) for a in aways)

        def both_halves(value, theirs, axis):
            odd = (place & 1) != 0
            return jnp.concatenate(
                [jnp.where(odd, theirs, value), jnp.where(odd, value, theirs)], axis
            ).astype(WIDE)

    else:
        grad_reduce = weight_grad(activated, cot_all, 1)
        grad_expand = weight_grad(normed_two, grad_expanded, 0)

    mine_grads = spread_context(grad_piece)
    out_near, out_far = last_terms(after(out_keep, grad_piece), after(out_send, grad_piece))
    ready = [out_far]
    theirs = [swap(m, "tensor", 1) for m in mine_grads[:1]]
    if pair:
        reduce_half = pin((dot_lt(act_half, cot_own) + reduce_got.astype(WIDE)).astype(LOW))
        mine_grads[1:] = lax.optimization_barrier((*mine_grads[1:], reduce_got))[:-1]
        expand_own = pin(dot_lt(after(normed_own, grad_piece), grad_expanded))
        ready += [reduce_half, expand_own]
    theirs += [swap(m, "tensor", 1) for m in mine_grads[1:]]
    grad_branch, grad_qkv, keep, send, branch_sum, norm_sums, head_sum, away = kernel(
        lambda *refs: attend_back_body(heads, head_dim, blocks, parts, *refs),
        (
            low(length, width),
            low(length, 3 * features),
            low(half, width),
            low(half, width),
            wide(1, width),
            wide(2, width),
            wide(1, 3 * features),
            low(width // parts, 4 * features),
        ),
        *woven(mine_grads, theirs),
        *output_parts,
        after(qkv, *ready),
        *packed,
        normed_all,
        context_own,
        context_rest,
        count=valid_count,
        flops=10 * length * length * features,
        moved=8 * length * width,
    )
    if pair:
        qkv_got = across(away)
    if pair:
        send = after(send, expand_got)
    near, far = last_terms(keep, send)
    gn_far = far
    if pair:
        reduce_theirs = swap(after(reduce_half, near), "context", 1)
        grad_expand = expand_own + expand_got.astype(WIDE)
    grad_token_piece = kernel(
        first_back_body, wide(half, width), near, far, own_piece, grad_hidden, vec
    )

    def both_cores(value):
        theirs = swap(value, "tensor", 1)
        upper = core == 1
        return turned(
            jnp.concatenate([jnp.where(upper, theirs, value), jnp.where(upper, value, theirs)], 0)
        ).reshape(tokens.shape)

    grad_tokens = both_cores(grad_token_piece)

    reduced = out_near.astype(WIDE) + out_far.astype(WIDE) + vec[5:6, :]
    output = both_cores((hidden + reduced).astype(LOW))

    if not pair:
        grad_weights = scatter(dot_lt(normed_all, grad_qkv), 0).astype(WIDE)
        grad_query, grad_key, grad_value = jnp.split(grad_weights, 3, 1)
        context_all = jnp.concatenate([context_own, context_rest], 0)
        grad_output = scatter(dot_lt(context_all, grad_branch), 1).astype(WIDE)

    first_sums = kernel(
        lambda *refs: first_sums_body(parts, *refs), wide(2, width), after(grad_qkv, gn_far), xhat_all, *packed
    )
    bit = 1
    while bit < lax.axis_size("tensor"):
        first_sums = first_sums + swap(first_sums, "tensor", bit)
        bit *= 2
    if pair:
        grad_reduce = both_halves(reduce_half, reduce_theirs, 0)
    sums = jnp.concatenate([first_sums, norm_sums, branch_sum, cot_sum], 0)
    plain = jnp.concatenate(
        [jnp.pad(head_sum, ((0, 0), (0, width - 3 * features))), unit_sum], 0
    )
    if pair:
        own, other = segments(sums, 2)
        lines = across(jnp.concatenate([other, *segments(plain, 2)], 0))
        grads = kernel(
            last_body,
            (wide(share, features),) * 3
            + (wide(features, share),)
            + (wide(share),) * 6
            + (wide(heads, head_dim // 2),) * 2
            + (wide(expand_bias.shape[1], expand_bias.shape[0]),),
            after(dot_lt(segments(after(normed_all, gn_far), 2)[0], grad_qkv), grad_tokens, output, grad_reduce),
            dot_lt(
                jnp.concatenate([context_own, context_rest], 0),
                segments(after(grad_branch, gn_far), 2)[0],
            ),
            qkv_got,
            own,
            plain,
            lines,
        )
        grad_query, grad_key, grad_value, grad_output, *sums = grads[:10]
        grad_qbias, grad_vbias, grad_ebias = (g.T for g in grads[10:])
    else:
        sums = scatter(sums, 1).astype(WIDE)
        plain = lax.psum(plain, "fsdp")

        def own_rows(value):
            size = value.shape[0] // ways
            return lax.dynamic_slice_in_dim(value, mine * size, size, 0)

        grad_ebias = own_rows(plain[1].reshape(-1, expand_bias.shape[0] * ways).T)
        grad_qbias, grad_vbias = (
            own_rows(plain[0, n * features : (n + 1) * features].reshape(heads, head_dim).T)
            for n in (0, 2)
        )
    return (
        output,
        grad_tokens,
        sums[0],
        sums[1],
        grad_query,
        grad_qbias,
        grad_key,
        grad_value,
        grad_vbias,
        grad_output,
        sums[4],
        sums[2],
        sums[3],
        grad_expand,
        grad_ebias,
        grad_reduce,
        sums[5],
    )


def solution(mesh):
    rows = P("fsdp", "context", None)
    vector = P("fsdp")
    split = P("fsdp", "tensor")
    turned = P("tensor", "fsdp")
    in_specs = (rows, rows, vector, vector, vector, split, split, split, split, split)
    in_specs += (turned, vector, vector, vector, split, split, turned, vector)
    out_specs = (rows, rows, vector, vector, split, split, split, split, split)
    out_specs += (turned, vector, vector, vector, split, split, turned, vector)
    return jax.shard_map(
        on_device, mesh=mesh, in_specs=in_specs, out_specs=out_specs, check_vma=False
    )
```
